32 devices in a mesh: groups: 2 (over x), blk: 8 (over z, y), tensor: 2 (over core).
Axes of the slice: x: 2, y: 2, z: 4, core: 2. Of those that a mesh axis runs over, the one named last changes fastest.
Arguments:
- queries: bfloat16 [2048, 8192], P(('groups', 'blk'), 'tensor'), parts along dimension 0, may hold values from -64 to 64
- new_keys: bfloat16 [2048, 1024], P(('groups', 'blk'), 'tensor'), parts along dimension 0, may hold values from -24 to 24
- new_values: bfloat16 [2048, 1024], P(('groups', 'blk'), 'tensor'), parts along dimension 0, may hold values from -6 to 6
- prefix_keys: bfloat16 [2048, 1024], P(('groups', 'blk'), 'tensor'), parts along dimension 0, may hold values from -24 to 24
- prefix_values: bfloat16 [2048, 1024], P(('groups', 'blk'), 'tensor'), parts along dimension 0, may hold values from -6 to 6
- span_lens: int32 [4], P('groups'), parts along dimension 0, may hold values from 1 to 768, 1024 in all
- prefix_lens: int32 [4], P('groups'), parts along dimension 0, may hold values from 1 to 640, 1024 in all
- placement: int32 [2048], P('groups'), parts along dimension 0, may hold values from 0 to 1023, as said below
- decode_dest: int32 [2048, 1], P('groups'), parts along dimension 0, may hold values from 0 to 7; in each aligned block of 128 rows (0 to 127, 128 to 255, ...) at most 32 rows name the same one
Outputs:
- attended: bfloat16 [2048, 8192], P(('groups', 'blk'), 'tensor'), parts along dimension 0
- decode_keys: bfloat16 [4096, 1024], P(('groups', 'blk'), 'tensor'), parts along dimension 0
- decode_values: bfloat16 [4096, 1024], P(('groups', 'blk'), 'tensor'), parts along dimension 0
The draws below stay inside these ranges and needn't reach their ends.
There are 2 independent parts, one for each index of `groups`. The reference program is written for one: setup_inputs(seed, part) draws one part's arguments, and reference() takes and returns one part's arrays. A program takes and returns all parts, laid end to end along the dimension named above; each array names one. Nothing has to cross between parts.
Inputs may be any that keep to these rules, and one draw needn't show every extreme that they name: `placement`: each aligned run of 64 slots holds 64 consecutive tokens in rising order; every token has exactly one slot. `decode_dest`: among the 128 slots of one cycle instance at most 32 go to any one decode instance, and in every draw some instance sends exactly 32 to some decode instance.
All inputs are finite; a program needn't handle non-finite values.
Results may differ from the reference program's by a relative error of at most 0.006.
Values may be sent and summed in bfloat16 or wider, within the bound.
No kernel may reach another device: no remote copies, remote signals or barrier semaphores. Data moves between devices by JAX's collectives and lax.ppermute only.
A program may use at most 128 MiB of HBM per device.

```python
import math
import jax
import jax.numpy as jnp
import numpy as np
from jax import lax

H = 64
KVH = 8
HD = 128
TOK_DEV = 128
REQS = 2
CYCLE = 8
TOKENS = 1024
PREFIX = 1024
PIECE = 64
CAP = 32
DEC_ROWS = 2048


def base_field(key, shape):
    return jnp.clip(jax.random.normal(key, shape, jnp.float32), -6.0, 6.0)


def draw_queries(key, part):
    key = jax.random.fold_in(key, 1)
    field = base_field(key, (TOKENS, H, HD))
    return field.reshape(TOKENS, H * HD).astype(jnp.bfloat16)


def draw_new_keys(key, part):
    key = jax.random.fold_in(key, 2)
    field = base_field(key, (TOKENS, KVH, HD))
    return field.reshape(TOKENS, KVH * HD).astype(jnp.bfloat16)


def draw_prefix_keys(key, part):
    key = jax.random.fold_in(key, 3)
    field = base_field(key, (PREFIX, KVH, HD))
    return field.reshape(PREFIX, KVH * HD).astype(jnp.bfloat16)


def draw_placement(key, part):
    key = jax.random.fold_in(key, 4)
    runs = TOKENS // PIECE
    order = jax.random.permutation(key, runs).astype(jnp.int32)
    slots = jnp.arange(TOKENS, dtype=jnp.int32)
    return (order[slots // PIECE] * PIECE + slots % PIECE).astype(jnp.int32)


def shard_levels(own_key, dims, shards, smallest, high):
    factor_of = 1.0
    for axis_at, parts in shards:
        steps = jax.random.uniform(jax.random.fold_in(jax.random.fold_in(own_key, 6), axis_at), (parts,), jnp.float32, smallest / len(shards), high / len(shards))
        factor_of = factor_of * jnp.repeat(jnp.exp(steps), dims[axis_at] // parts).reshape((-1,) + (1,) * (len(dims) - 1 - axis_at))
    return factor_of


def length_profile(number_of, total, bound, lean):
    weights = [(1 << 20) // math.isqrt(rank ** lean) + 1 for rank in range(2, number_of + 1)]
    spare, given = total - bound - (number_of - 1), [1] * (number_of - 1)
    while spare > 0:
        movable = [i for i in range(number_of - 1) if given[i] < bound]
        pool, remaining = sum([weights[i] for i in movable]), spare
        for i in movable:
            extra = min(bound - given[i], max(1, remaining * weights[i] // pool), spare)
            given[i] = given[i] + extra
            spare = spare - extra
    return np.array([bound] + given)


def uneven(stream_key, amount, total, reach, lean):
    if amount == 2:
        one = jax.random.randint(stream_key, (), max(1, total - reach), min(reach, total - 1) + 1)
        return jnp.stack([one, total - one])
    sizes = jnp.asarray(length_profile(amount, total, reach, lean), jnp.int32)
    pairs = (amount - 1) // 2
    donor, sink = sizes[1:1 + 2 * pairs:2], sizes[2:2 + 2 * pairs:2]
    room = jnp.minimum(donor - 1, reach - sink)
    moved = jax.random.randint(jax.random.fold_in(stream_key, 1), (pairs,), 0, 1 << 20) % (room + 1)
    sizes = sizes.at[1:1 + 2 * pairs:2].set(donor - moved).at[2:2 + 2 * pairs:2].set(sink + moved)
    return sizes[jax.random.permutation(jax.random.fold_in(stream_key, 2), amount)]


def assign_block(stream_key, own, number, rows, number_of, top, limit, skew):
    ranking = jax.random.permutation(stream_key, number_of)
    crowded, usual = portions_of(number_of, rows * top, limit, skew, True), portions_of(number_of, rows * top, limit, skew, False)
    places = jnp.arange(number_of)

    def named(sizes, rotation):
        used = int((sizes > 0).sum())
        fixed = max(1, used // 4)
        passed = fixed + (places - fixed + rotation * (used - fixed)) % max(1, number_of - fixed)
        return jnp.zeros((number_of,), jnp.int32).at[ranking[jnp.where(places < fixed, places, passed)]].set(jnp.asarray(sizes, jnp.int32))

    sizes = jnp.where(number % 4 == 0, named(crowded, number // 4), named(usual, number - number // 4 - 1))
    mixed = jax.random.permutation(jax.random.fold_in(own, 3), number_of)
    source_of, receiver = mixed[0:number_of // 2 * 2:2], mixed[1:number_of // 2 * 2:2]
    slack = jnp.minimum(sizes[source_of] - 1, limit - sizes[receiver]) // 2
    slack = jnp.where((source_of == ranking[0]) | (receiver == ranking[0]) | (sizes[receiver] == 0), 0, jnp.maximum(slack, 0))
    passed = jax.random.randint(jax.random.fold_in(own, 4), (number_of // 2,), 0, 1 << 20) % (slack + 1)
    sizes = sizes.at[source_of].add(-passed).at[receiver].add(passed)
    items = jnp.searchsorted(jnp.cumsum(sizes), jnp.arange(rows * top), side="right").astype(jnp.int32)
    listing = items.reshape(top, rows).T
    listing = listing[jax.random.permutation(jax.random.fold_in(own, 1), rows)]
    rotation = jax.random.randint(jax.random.fold_in(own, 2), (rows, 1), 0, top)
    return jnp.take_along_axis(listing, (jnp.arange(top)[None, :] + rotation) % top, axis=1)


def portions_of(amount, total, reach, lean, full):
    portions = [(1 << 20) // math.isqrt(standing ** lean) + 1 for standing in range(1, amount + 1)]
    largest = reach if full else min(reach, max(-(-total // amount), total * portions[0] // sum(portions)))
    least = 1 if total - largest >= amount - 1 else 0
    holding, rest = [largest] + [least] * (amount - 1), total - largest - least * (amount - 1)
    while rest > 0:
        movable = [i for i in range(1, amount) if holding[i] < largest] or [i for i in range(1, amount) if holding[i] < reach]
        mass, remaining = sum([portions[i] for i in movable]), rest
        for i in movable:
            addition = min(reach - holding[i], max(1, remaining * portions[i] // mass), rest)
            holding[i] = holding[i] + addition
            rest = rest - addition
    return np.array(holding)


def bell_draw(rng, extent, scale, reach, split=(), kind=jnp.bfloat16):
    array = scale * jax.random.normal(rng, extent, jnp.float32)
    if split:
        array = array * shard_levels(rng, extent, split, -0.22, 0.18)
    return jnp.clip(array, -reach, reach).astype(kind)


def setup_inputs(seed: int = 0, part: int = 0) -> dict:
    seeds = jax.random.split(jax.random.key(seed), 10)
    part_keys = jax.random.split(jax.random.fold_in(seeds[9], part), 10)
    queries = draw_queries(jax.random.fold_in(jax.random.fold_in(seeds[9], part), 71), part)
    new_keys = draw_new_keys(jax.random.fold_in(jax.random.fold_in(seeds[9], part), 71), part)
    new_values = bell_draw(part_keys[2], (TOKENS, KVH * HD), 1.0, 6.0, ((0, 8), (1, 2)))
    prefix_keys = draw_prefix_keys(jax.random.fold_in(jax.random.fold_in(seeds[9], part), 71), part)
    prefix_values = bell_draw(part_keys[4], (PREFIX, KVH * HD), 1.0, 6.0, ((0, 8), (1, 2)))
    span_lens = uneven(part_keys[5], REQS, TOKENS, 3 * TOKENS // 4, 2).astype(jnp.int32)
    prefix_lens = uneven(part_keys[6], REQS, PREFIX, 5 * PREFIX // 8, 2).astype(jnp.int32)
    placement = draw_placement(jax.random.fold_in(jax.random.fold_in(seeds[9], part), 71), part)
    decode_dest_keys = jax.random.split(jax.random.fold_in(part_keys[8], 1), TOKENS // TOK_DEV)
    decode_dest_turns = jax.random.permutation(jax.random.fold_in(part_keys[8], 3), TOKENS // TOK_DEV)
    decode_dest = jax.vmap(lambda own, number: assign_block(jax.random.fold_in(part_keys[8], 2), own, number, TOK_DEV, CYCLE, 1, CAP, 2))(decode_dest_keys, decode_dest_turns).reshape((TOKENS, 1))
    return {"queries": queries, "new_keys": new_keys, "new_values": new_values, "prefix_keys": prefix_keys, "prefix_values": prefix_values, "span_lens": span_lens, "prefix_lens": prefix_lens, "placement": placement, "decode_dest": decode_dest}


masked_score = -1e+30

def request_of(index, lens):
    ends = jnp.cumsum(lens).astype(jnp.int32)
    return lax.optimization_barrier(jnp.sum((index[:, None] >= ends[None, :]).astype(jnp.int32), axis=1)).astype(jnp.int32)

def reference(queries, new_keys, new_values, prefix_keys, prefix_values, span_lens, prefix_lens, placement, decode_dest):
    score_scale = 1.0 / math.sqrt(HD)
    groups = H // KVH
    tok_req = request_of(placement, span_lens)
    pre_req = request_of(jnp.arange(PREFIX, dtype=jnp.int32), prefix_lens)
    key_req = jnp.concatenate([pre_req, tok_req]).astype(jnp.int32)
    key_tok = jnp.concatenate([jnp.full((PREFIX,), -1, jnp.int32), placement.astype(jnp.int32)])
    all_keys = jnp.concatenate([prefix_keys, new_keys]).astype(jnp.float32).reshape(-1, KVH, HD).transpose(1, 0, 2)
    all_values = jnp.concatenate([prefix_values, new_values]).astype(jnp.float32).reshape(-1, KVH, HD).transpose(1, 0, 2)
    blocks = TOKENS // TOK_DEV
    query_blocks = queries.reshape(blocks, TOK_DEV, KVH, groups, HD)
    req_blocks = tok_req.reshape(blocks, TOK_DEV)
    tok_blocks = placement.reshape(blocks, TOK_DEV)

    def one_block(items):
        query_part, req_part, tok_part = items
        visible = (key_req[None, :] == req_part[:, None]) & (key_tok[None, :] <= tok_part[:, None])

        def one_head(head_items):
            query_head, key_head, value_head = head_items
            scores = jnp.einsum('tgd,nd->gtn', query_head.astype(jnp.float32), key_head) * score_scale
            scores = jnp.where(visible[None], scores, masked_score)
            largest = lax.optimization_barrier(jnp.max(scores, axis=-1, keepdims=True))
            weights = jnp.where(visible[None], jnp.exp(scores - largest), 0.0)
            totals = lax.optimization_barrier(jnp.sum(weights, axis=-1))
            rounded = lax.optimization_barrier(weights.astype(jnp.bfloat16)).astype(jnp.float32)
            numer = jnp.einsum('gtn,nd->gtd', rounded, value_head)
            return numer / totals[..., None]
        heads_out = lax.map(one_head, (query_part.transpose(1, 0, 2, 3), all_keys, all_values))
        return heads_out.transpose(2, 0, 1, 3).reshape(TOK_DEV, H * HD).astype(jnp.bfloat16)
    attended = lax.map(one_block, (query_blocks, req_blocks, tok_blocks)).reshape(TOKENS, H * HD)
    destination = decode_dest[:, 0].astype(jnp.int32)
    source = (jnp.arange(TOKENS, dtype=jnp.int32) // TOK_DEV).astype(jnp.int32)
    one_hot = (destination[:, None] == jnp.arange(CYCLE, dtype=jnp.int32)[None, :]).astype(jnp.int32)
    running = jnp.cumsum(one_hot.reshape(CYCLE, TOK_DEV, CYCLE), axis=1).reshape(TOKENS, CYCLE)
    slot_rank = lax.optimization_barrier(jnp.sum(running * one_hot, axis=1)).astype(jnp.int32) - 1
    target = (destination * (CYCLE * CAP) + source * CAP + slot_rank).astype(jnp.int32)
    stacked = jnp.concatenate([new_keys, new_values], axis=1).astype(jnp.float32)
    caches = jnp.zeros((DEC_ROWS, 2 * KVH * HD), jnp.float32).at[target].set(stacked).astype(jnp.bfloat16)
    return (attended, caches[:, :KVH * HD], caches[:, KVH * HD:])
```

```python
import functools
import math

import jax
import jax.numpy as jnp
from jax import lax
from jax.experimental import pallas as pl
from jax.experimental.pallas import tpu as pltpu
from jax.sharding import PartitionSpec as P

H = 64
KVH = 8
HD = 128
PIECE = 64
LARGE_NEGATIVE = -1e30

VMEM = pltpu.VMEM
SMEM = pltpu.SMEM
ANY = pl.ANY


def dot_nt(a, b):
    return lax.dot_general(a, b, (((1,), (1,)), ((), ())), preferred_element_type=jnp.float32)


def dot_nn(a, b):
    return lax.dot_general(a, b, (((1,), (0,)), ((), ())), preferred_element_type=jnp.float32)


def stage_kernel(offsets, parts, first, last, rows, heads, groups, requests, capacity, *refs):
    refs = list(refs)
    me_ref, place_ref, span_ref, plen_ref, dest_ref, query_ref = refs[:6]
    refs = refs[6:]
    blocks = []
    for count in parts:
        blocks.append(refs[:count])
        refs = refs[count:]
    if not first:
        max_in, acc_in = refs[:2]
        refs = refs[4:]
    if last:
        att_ref, dkey_ref, dval_ref = refs[:3]
        refs = refs[3:]
        max_ref, acc_ref = max_in, acc_in
    else:
        max_ref, acc_ref, dkey_ref, dval_ref = refs[:4]
        refs = refs[4:]
    picked_ref, sems = refs
    me = me_ref[0]
    pieces = rows // PIECE
    unit = groups * PIECE
    factor = math.log2(math.e) / math.sqrt(HD)

    def bounds(token):
        low = jnp.zeros_like(token)
        pre_low = jnp.zeros_like(token)
        pre_high = jnp.zeros_like(token) + plen_ref[0]
        end = jnp.int32(0)
        for r in range(requests - 1):
            end = end + span_ref[r]
            past = token >= end
            low = low + jnp.where(past, span_ref[r], 0)
            pre_low = pre_low + jnp.where(past, plen_ref[r], 0)
            pre_high = pre_high + jnp.where(past, plen_ref[r + 1], 0)
        return low, pre_low, pre_high

    def part_of(block, which, start, size):
        if len(block) == 1:
            return block[0][which * rows:(which + 1) * rows, pl.ds(start, size)]
        half, inner = divmod(which, 2)
        return block[half][inner * rows:(inner + 1) * rows, pl.ds(start, size)]

    copies = []
    for n, (offset, block) in enumerate(zip(offsets, blocks)):
        index = me ^ offset
        for piece in range(pieces):
            base = place_ref[me * rows + piece * PIECE]
            low0, pre0, unused = bounds(base)
            unused, unused2, pre1 = bounds(base + (PIECE - 1))
            seen = (pre0 < (index + 1) * rows) & (pre1 > index * rows)
            for other in range(pieces):
                there = place_ref[index * rows + other * PIECE]
                seen = seen | ((there <= base) & (there + (PIECE - 1) >= low0))

            def work(piece=piece, base=base, block=block, index=index, n=n):
                token = base + lax.broadcasted_iota(jnp.int32, (PIECE, 1), 0)
                low, pre_low, pre_high = bounds(token)
                column = lax.broadcasted_iota(jnp.int32, (PIECE, rows), 1)
                position = column + index * rows
                pre_seen = (position >= pre_low) & (position < pre_high)
                key_token = jnp.zeros((PIECE, rows), jnp.int32)
                for other in range(pieces):
                    there = place_ref[index * rows + other * PIECE] - other * PIECE
                    key_token = jnp.where(column >= other * PIECE, column + there, key_token)
                new_seen = (key_token >= low) & (key_token <= token)
                bias = jnp.concatenate(
                    [
                        jnp.where(pre_seen, 0.0, LARGE_NEGATIVE),
                        jnp.where(new_seen, 0.0, LARGE_NEGATIVE),
                    ],
                    axis=1,
                ).astype(jnp.float32)
                step = 4
                for k in range(heads):
                    keys = jnp.concatenate(
                        [part_of(block, 0, k * HD, HD), part_of(block, 2, k * HD, HD)], axis=0
                    )
                    values = jnp.concatenate(
                        [part_of(block, 1, k * HD, HD), part_of(block, 3, k * HD, HD)], axis=0
                    )
                    values = jnp.concatenate([values, jnp.ones_like(values)], axis=1)
                    for g in range(0, groups, step):
                        query = jnp.concatenate(
                            [
                                query_ref[
                                    piece * PIECE:(piece + 1) * PIECE,
                                    (k * groups + g + j) * HD:(k * groups + g + j + 1) * HD,
                                ]
                                for j in range(step)
                            ],
                            axis=0,
                        )
                        scores = dot_nt(query, keys) * factor
                        scores = scores.reshape(step, PIECE, 2 * rows) + bias[None]
                        scores = scores.reshape(step * PIECE, 2 * rows)
                        at = slice(g * PIECE, (g + step) * PIECE)
                        here = jnp.max(scores, axis=1, keepdims=True)
                        if first and n == 0:
                            new_max = jnp.broadcast_to(here, (step * PIECE, HD))
                        else:
                            source_max, source_acc = (
                                (max_in, acc_in) if n == 0 and not first else (max_ref, acc_ref)
                            )
                            old_max = source_max[k, piece, at, :]
                            new_max = jnp.maximum(old_max, here)
                        weights = jnp.exp2(scores - jnp.concatenate([new_max, new_max], axis=1))
                        added = dot_nn(weights.astype(jnp.bfloat16), values)
                        if not (first and n == 0):
                            rescale = jnp.exp2(old_max - new_max)
                            rescale = jnp.concatenate([rescale, rescale], axis=1)
                            added = source_acc[k, piece, at, :] * rescale + added
                        acc_ref[k, piece, at, :] = added
                        max_ref[k, piece, at, :] = new_max

            if first and n == 0:
                work()
            else:
                pl.when(seen)(work)
        mine = jnp.where(dest_ref[pl.ds(index, 1), :] == me, 1.0, 0.0)
        lane = lax.broadcasted_iota(jnp.int32, (rows, rows), 0)
        lane2 = lax.broadcasted_iota(jnp.int32, (rows, rows), 1)
        earlier = jnp.where(lane < lane2, 1.0, 0.0).astype(jnp.bfloat16)
        mine = jnp.broadcast_to(mine, (capacity, rows))
        rank = dot_nn(mine.astype(jnp.bfloat16), earlier)
        slot = lax.broadcasted_iota(jnp.int32, (capacity, rows), 0).astype(jnp.float32)
        choose = jnp.where((rank == slot) & (mine > 0.5), 1.0, 0.0).astype(jnp.bfloat16)
        for which, out_ref in ((2, dkey_ref), (3, dval_ref)):
            picked_ref[n, which - 2] = dot_nn(choose, part_of(block, which, 0, heads * HD)).astype(
                jnp.bfloat16
            )
            copy = pltpu.make_async_copy(
                picked_ref.at[n, which - 2],
                out_ref.at[pl.ds(pl.multiple_of(index * capacity, capacity), capacity)],
                sems.at[n, which - 2],
            )
            copy.start()
            copies.append(copy)
    if last:
        for piece in range(pieces):
            for k in range(heads):
                for g in range(groups):
                    both = acc_ref[k, piece, g * PIECE:(g + 1) * PIECE, :]
                    att_ref[
                        piece * PIECE:(piece + 1) * PIECE,
                        (k * groups + g) * HD:(k * groups + g + 1) * HD,
                    ] = (both[:, :HD] / both[:, HD:]).astype(jnp.bfloat16)
    for copy in copies:
        copy.wait()


def run_stage(common, offsets, blocks, carry, last, capacity):
    query = common[-1]
    rows, columns = query.shape
    groups = H // KVH
    heads = columns // (groups * HD)
    requests = common[2].shape[0]
    pieces = rows // PIECE
    first = carry is None
    parts = tuple(len(block) for block in blocks)
    flat = [ref for block in blocks for ref in block]
    operands = list(common) + flat + (list(carry) if carry is not None else [])
    specs = [pl.BlockSpec(memory_space=SMEM)] * 4 + [pl.BlockSpec(memory_space=VMEM)] * (2 + len(flat))
    unit = groups * PIECE
    max_shape = jax.ShapeDtypeStruct((heads, pieces, unit, HD), jnp.float32)
    acc_shape = jax.ShapeDtypeStruct((heads, pieces, unit, 2 * HD), jnp.float32)
    decode_shape = jax.ShapeDtypeStruct((capacity * (common[1].shape[0] // rows), heads * HD), jnp.bfloat16)
    alias = {}
    at = len(common) + len(flat)
    if not first:
        specs += [pl.BlockSpec(memory_space=VMEM)] * 2 + [pl.BlockSpec(memory_space=ANY)] * 2
    if last:
        out_shape = (jax.ShapeDtypeStruct((rows, columns), jnp.bfloat16), decode_shape, decode_shape)
        out_specs = (pl.BlockSpec(memory_space=VMEM),) + (pl.BlockSpec(memory_space=ANY),) * 2
        alias = {at + 2: 1, at + 3: 2}
    else:
        out_shape = (max_shape, acc_shape, decode_shape, decode_shape)
        out_specs = (pl.BlockSpec(memory_space=VMEM),) * 2 + (pl.BlockSpec(memory_space=ANY),) * 2
        if not first:
            alias = {at + j: j for j in range(4)}
    body = functools.partial(
        stage_kernel, offsets, parts, first, last, rows, heads, groups, requests, capacity
    )
    keys = 2 * rows * len(blocks)
    return pl.pallas_call(
        body,
        out_shape=out_shape,
        in_specs=specs,
        out_specs=out_specs,
        input_output_aliases=alias,
        scratch_shapes=[
            VMEM((len(blocks), 2, capacity, heads * HD), jnp.bfloat16),
            pltpu.SemaphoreType.DMA((len(blocks), 2)),
        ],
        compiler_params=pltpu.CompilerParams(vmem_limit_bytes=20 * 1024 * 1024),
        cost_estimate=pl.CostEstimate(
            flops=4 * rows * columns * keys, bytes_accessed=4 * 1024 * 1024, transcendentals=0
        ),
    )(*operands)


def together(values, *after):
    return lax.optimization_barrier(tuple(values) + after)[: len(values)]


def cycle_of_eight(
    queries, new_keys, new_values, prefix_keys, prefix_values, span_lens, prefix_lens, placement, decode_dest
):
    cycle = lax.axis_size("blk")
    me = lax.axis_index("blk")
    rows = queries.shape[0]
    capacity = 2 * rows // cycle
    place = me // 2
    outer = (place == 0) | (place == 3)

    def moves(table):
        return [(2 * a + y, 2 * b + y) for a, b in table.items() for y in range(2)]

    swap = [(i, i ^ 1) for i in range(cycle)]
    near = moves({0: 1, 1: 0, 2: 3, 3: 2})
    middle = moves({1: 2, 2: 1})
    ends = moves({0: 3, 3: 0})
    skip = moves({0: 2, 3: 1, 2: 3, 1: 0})
    send = lambda x, table: lax.ppermute(x, "blk", table)

    common = (
        me.astype(jnp.int32)[None],
        placement,
        span_lens,
        prefix_lens,
        decode_dest.reshape(cycle, rows),
        queries,
    )
    own = jnp.concatenate([prefix_keys, prefix_values, new_keys, new_values], axis=0)
    half = own.shape[0] // 2

    a = send(own, near)
    y_own = send(own, swap)
    b_inner = send(own, middle)
    carry = run_stage(common, (0,), [[own]], None, False, capacity)

    own_2, a_2, y_own_2, *carry = together((own, a, y_own) + tuple(carry))
    b_outer = send(own_2, ends)
    y_a = send(a_2, swap)
    carry = run_stage(common, (2, 1), [[a_2], [y_own_2]], carry, False, capacity)

    b = jnp.where(outer, b_outer, b_inner)
    skip_from, b, y_a, *carry = together((jnp.where(outer, own_2, b_inner), b, y_a) + tuple(carry))
    c = send(skip_from, skip)
    y_b = send(b, swap)
    carry = run_stage(common, (6, 3), [[b], [y_a]], carry, False, capacity)

    c, y_b, *carry = together((c, y_b) + tuple(carry))
    y_c_low = send(c[:half], swap)
    y_c_high = send(y_b[half:], near)
    carry = run_stage(common, (4, 7), [[c], [y_b]], carry, False, capacity)
    return run_stage(common, (5,), [[y_c_low, y_c_high]], carry, True, capacity)


masked_score = -1e30


def request_of(index, lens):
    ends = jnp.cumsum(lens)
    return jnp.sum((index[:, None] >= ends[None, :]).astype(jnp.int32), axis=1)


def block_rows_for(length):
    chosen = 512
    while length % chosen:
        chosen = chosen // 2
    return chosen


def attend(carried, query_groups, query_req, query_tok, keys, values, key_req, key_tok):
    length = keys.shape[0]
    chosen = block_rows_for(length)
    blocks = length // chosen
    heads_here = query_groups.shape[1]
    score_scale = 1.0 / math.sqrt(HD)
    key_blocks = keys.reshape(blocks, chosen, heads_here, HD)
    value_blocks = values.reshape(blocks, chosen, heads_here, HD)
    req_blocks = key_req.reshape(blocks, chosen)
    tok_blocks = key_tok.reshape(blocks, chosen)

    def one_block(inner, items):
        running_max, running_sum, numerator = inner
        key_part, value_part, req_part, tok_part = items
        visible = (req_part[None, :] == query_req[:, None]) & (
            tok_part[None, :] <= query_tok[:, None]
        )
        scores = (
            jnp.einsum("tkgd,nkd->kgtn", query_groups, key_part, preferred_element_type=jnp.float32)
            * score_scale
        )
        scores = jnp.where(visible, scores, masked_score)
        new_max = jnp.maximum(running_max, jnp.max(scores, axis=-1))
        rescale = jnp.exp(running_max - new_max)
        weights = jnp.where(visible, jnp.exp(scores - new_max[..., None]), 0.0)
        running_sum = running_sum * rescale + jnp.sum(weights, axis=-1)
        numerator = numerator * rescale[..., None] + jnp.einsum(
            "kgtn,nkd->kgtd",
            weights.astype(jnp.bfloat16),
            value_part,
            preferred_element_type=jnp.float32,
        )
        return ((new_max, running_sum, numerator), None)

    result, ignored = lax.scan(
        one_block, carried, (key_blocks, value_blocks, req_blocks, tok_blocks)
    )
    return result


def maybe_attend(
    carried, query_groups, query_req, query_tok, summary, keys, values, key_req, key_tok
):
    query_has, query_last = summary
    request_ids = jnp.arange(query_has.shape[0], dtype=jnp.int32)
    matches = key_req[:, None] == request_ids[None, :]
    wanted = jnp.any(matches & query_has[None, :], axis=1)
    latest = jnp.max(jnp.where(matches, query_last[None, :], -2), axis=1)
    touched = jnp.any(wanted & (key_tok <= latest))
    return lax.cond(
        touched,
        lambda inner: attend(
            inner, query_groups, query_req, query_tok, keys, values, key_req, key_tok
        ),
        lambda inner: inner,
        carried,
    )


def any_cycle(
    queries,
    new_keys,
    new_values,
    prefix_keys,
    prefix_values,
    span_lens,
    prefix_lens,
    placement,
    decode_dest,
):
    cycle_size = lax.axis_size("blk")
    my_index = lax.axis_index("blk")
    rows_here = queries.shape[0]
    kv_cols = new_keys.shape[1]
    heads_here = kv_cols // HD
    groups = H // KVH
    query_groups = queries.reshape(rows_here, heads_here, groups, HD)
    query_tok = lax.dynamic_slice_in_dim(placement, my_index * rows_here, rows_here)
    query_req = request_of(query_tok, span_lens)
    token_req = request_of(placement, span_lens)
    prefix_total = prefix_keys.shape[0] * cycle_size
    prefix_req = request_of(jnp.arange(prefix_total, dtype=jnp.int32), prefix_lens)
    request_ids = jnp.arange(span_lens.shape[0], dtype=jnp.int32)
    member = query_req[:, None] == request_ids[None, :]
    summary = (jnp.any(member, axis=0), jnp.max(jnp.where(member, query_tok[:, None], -1), axis=0))
    initial = (
        jnp.full((heads_here, groups, rows_here), masked_score, jnp.float32),
        jnp.zeros((heads_here, groups, rows_here), jnp.float32),
        jnp.zeros((heads_here, groups, rows_here, HD), jnp.float32),
    )
    piece_keys = lax.all_gather(prefix_keys, "blk", axis=0, tiled=True)
    piece_values = lax.all_gather(prefix_values, "blk", axis=0, tiled=True)
    length = piece_keys.shape[0]
    key_req = prefix_req
    key_tok = jnp.full((length,), -1, jnp.int32)
    carried = maybe_attend(
        initial,
        query_groups,
        query_req,
        query_tok,
        summary,
        piece_keys,
        piece_values,
        key_req,
        key_tok,
    )
    destination = decode_dest[:, 0]
    capacity = 2 * rows_here // cycle_size
    piece_keys = lax.all_gather(new_keys, "blk", axis=0, tiled=True)
    piece_values = lax.all_gather(new_values, "blk", axis=0, tiled=True)
    key_req = token_req
    key_tok = placement
    carried = maybe_attend(
        carried,
        query_groups,
        query_req,
        query_tok,
        summary,
        piece_keys,
        piece_values,
        key_req,
        key_tok,
    )
    local_dest = lax.dynamic_slice_in_dim(destination, my_index * rows_here, rows_here)
    one_hot = (local_dest[:, None] == jnp.arange(cycle_size, dtype=jnp.int32)[None, :]).astype(
        jnp.int32
    )
    slot_rank = jnp.sum(jnp.cumsum(one_hot, axis=0) * one_hot, axis=1) - 1
    target = local_dest * capacity + slot_rank
    selector = (
        jnp.arange(cycle_size * capacity, dtype=jnp.int32)[:, None] == target[None, :]
    ).astype(jnp.bfloat16)
    stacked = jnp.concatenate([new_keys, new_values], axis=1)
    outgoing = jnp.dot(selector, stacked, preferred_element_type=jnp.float32).astype(jnp.bfloat16)
    moved = lax.all_to_all(outgoing, "blk", split_axis=0, concat_axis=0, tiled=True)
    running_max, running_sum, numerator = carried
    attended = (
        (numerator / running_sum[..., None])
        .transpose(2, 0, 1, 3)
        .reshape(rows_here, heads_here * groups * HD)
        .astype(jnp.bfloat16)
    )
    return (attended, moved[:, :kv_cols], moved[:, kv_cols:])


def solution(mesh):
    rows = P(("groups", "blk"), "tensor")
    return jax.shard_map(
        cycle_of_eight if mesh.shape["blk"] == 8 else any_cycle,
        mesh=mesh,
        in_specs=(rows,) * 5 + (P("groups"),) * 3 + (P("groups", None),),
        out_specs=(rows,) * 3,
        check_vma=False,
    )
```

```python
import functools
import math

import jax
import jax.numpy as jnp
from jax import lax
from jax.experimental import pallas as pl
from jax.experimental.pallas import tpu as pltpu
from jax.sharding import PartitionSpec as P

H = 64
KVH = 8
HD = 128
PIECE = 64
LARGE_NEGATIVE = -1e30

VMEM = pltpu.VMEM
SMEM = pltpu.SMEM
HBM = pltpu.HBM


def dot_nt(a, b):
    return lax.dot_general(a, b, (((1,), (1,)), ((), ())), preferred_element_type=jnp.float32)


def dot_nn(a, b):
    return lax.dot_general(a, b, (((1,), (0,)), ((), ())), preferred_element_type=jnp.float32)


def stage_kernel(offsets, parts, first, last, rows, heads, groups, requests, capacity, *refs):
    refs = list(refs)
    small_in, query_ref = refs[:4], refs[4]
    refs = refs[5:]
    blocks = []
    for count in parts:
        blocks.append(refs[:count])
        refs = refs[count:]
    if not first:
        max_in, acc_in = refs[:2]
        refs = refs[4:]
    if last:
        att_ref, dkey_ref, dval_ref = refs[:3]
        refs = refs[3:]
        max_ref, acc_ref = max_in, acc_in
    else:
        max_ref, acc_ref, dkey_ref, dval_ref = refs[:4]
        refs = refs[4:]
    if first:
        query_in, query_ref = query_ref, refs[0]
        refs = refs[1:]
    place_ref, span_ref, plen_ref, dest_ref, picked_ref, sems, small_sems = refs
    small = [
        pltpu.make_async_copy(source, target, small_sems.at[j])
        for j, (source, target) in enumerate(
            zip(small_in, (place_ref, span_ref, plen_ref, dest_ref))
        )
    ]
    if first:
        small.append(pltpu.make_async_copy(query_in, query_ref, small_sems.at[4]))
    for copy in small:
        copy.start()
    for copy in small:
        copy.wait()
    me = lax.axis_index("blk")
    pieces = rows // PIECE
    unit = groups * PIECE
    factor = math.log2(math.e) / math.sqrt(HD)

    def bounds(token):
        low = jnp.zeros_like(token)
        pre_low = jnp.zeros_like(token)
        pre_high = jnp.zeros_like(token) + plen_ref[0]
        end = jnp.int32(0)
        for r in range(requests - 1):
            end = end + span_ref[r]
            past = token >= end
            low = low + jnp.where(past, span_ref[r], 0)
            pre_low = pre_low + jnp.where(past, plen_ref[r], 0)
            pre_high = pre_high + jnp.where(past, plen_ref[r + 1], 0)
        return low, pre_low, pre_high

    def part_of(block, which, start, size):
        if len(block) == 1:
            return block[0][which * rows:(which + 1) * rows, pl.ds(start, size)]
        half, inner = divmod(which, 2)
        return block[half][inner * rows:(inner + 1) * rows, pl.ds(start, size)]

    copies = []
    for n, (offset, block) in enumerate(zip(offsets, blocks)):
        index = me ^ offset
        for piece in range(pieces):
            base = place_ref[me * rows + piece * PIECE]
            low0, pre0, unused = bounds(base)
            unused, unused2, pre1 = bounds(base + (PIECE - 1))
            seen = (pre0 < (index + 1) * rows) & (pre1 > index * rows)
            for other in range(pieces):
                there = place_ref[index * rows + other * PIECE]
                seen = seen | ((there <= base) & (there + (PIECE - 1) >= low0))

            def work(piece=piece, base=base, block=block, index=index, n=n):
                token = base + lax.broadcasted_iota(jnp.int32, (PIECE, 1), 0)
                low, pre_low, pre_high = bounds(token)
                column = lax.broadcasted_iota(jnp.int32, (PIECE, rows), 1)
                position = column + index * rows
                pre_seen = (position >= pre_low) & (position < pre_high)
                key_token = jnp.zeros((PIECE, rows), jnp.int32)
                for other in range(pieces):
                    there = place_ref[index * rows + other * PIECE] - other * PIECE
                    key_token = jnp.where(column >= other * PIECE, column + there, key_token)
                new_seen = (key_token >= low) & (key_token <= token)
                bias = jnp.concatenate(
                    [
                        jnp.where(pre_seen, 0.0, LARGE_NEGATIVE),
                        jnp.where(new_seen, 0.0, LARGE_NEGATIVE),
                    ],
                    axis=1,
                ).astype(jnp.float32)
                step = 4
                for k in range(heads):
                    keys = jnp.concatenate(
                        [part_of(block, 0, k * HD, HD), part_of(block, 2, k * HD, HD)], axis=0
                    )
                    values = jnp.concatenate(
                        [part_of(block, 1, k * HD, HD), part_of(block, 3, k * HD, HD)], axis=0
                    )
                    values = jnp.concatenate([values, jnp.ones_like(values)], axis=1)
                    for g in range(0, groups, step):
                        query = jnp.concatenate(
                            [
                                query_ref[
                                    piece * PIECE:(piece + 1) * PIECE,
                                    (k * groups + g + j) * HD:(k * groups + g + j + 1) * HD,
                                ]
                                for j in range(step)
                            ],
                            axis=0,
                        )
                        scores = dot_nt(query, keys) * factor
                        scores = scores.reshape(step, PIECE, 2 * rows) + bias[None]
                        scores = scores.reshape(step * PIECE, 2 * rows)
                        at = slice(g * PIECE, (g + step) * PIECE)
                        here = jnp.max(scores, axis=1, keepdims=True)
                        if first and n == 0:
                            new_max = jnp.broadcast_to(here, (step * PIECE, HD))
                        else:
                            source_max, source_acc = (
                                (max_in, acc_in) if n == 0 and not first else (max_ref, acc_ref)
                            )
                            old_max = source_max[k, piece, at, :]
                            new_max = jnp.maximum(old_max, here)
                        weights = jnp.exp2(scores - jnp.concatenate([new_max, new_max], axis=1))
                        added = dot_nn(weights.astype(jnp.bfloat16), values)
                        if not (first and n == 0):
                            rescale = jnp.exp2(old_max - new_max)
                            rescale = jnp.concatenate([rescale, rescale], axis=1)
                            added = source_acc[k, piece, at, :] * rescale + added
                        acc_ref[k, piece, at, :] = added
                        max_ref[k, piece, at, :] = new_max

            if first and n == 0:
                work()
            else:
                pl.when(seen)(work)
        mine = jnp.where(dest_ref[pl.ds(index, 1), :] == me, 1.0, 0.0)
        lane = lax.broadcasted_iota(jnp.int32, (rows, rows), 0)
        lane2 = lax.broadcasted_iota(jnp.int32, (rows, rows), 1)
        earlier = jnp.where(lane < lane2, 1.0, 0.0).astype(jnp.bfloat16)
        mine = jnp.broadcast_to(mine, (capacity, rows))
        rank = dot_nn(mine.astype(jnp.bfloat16), earlier)
        slot = lax.broadcasted_iota(jnp.int32, (capacity, rows), 0).astype(jnp.float32)
        choose = jnp.where((rank == slot) & (mine > 0.5), 1.0, 0.0).astype(jnp.bfloat16)
        for which, out_ref in ((2, dkey_ref), (3, dval_ref)):
            picked_ref[n, which - 2] = dot_nn(choose, part_of(block, which, 0, heads * HD)).astype(
                jnp.bfloat16
            )
            copy = pltpu.make_async_copy(
                picked_ref.at[n, which - 2],
                out_ref.at[pl.ds(pl.multiple_of(index * capacity, capacity), capacity)],
                sems.at[n, which - 2],
            )
            copy.start()
            copies.append(copy)
    if last:
        for piece in range(pieces):
            for k in range(heads):
                for g in range(groups):
                    both = acc_ref[k, piece, g * PIECE:(g + 1) * PIECE, :]
                    att_ref[
                        piece * PIECE:(piece + 1) * PIECE,
                        (k * groups + g) * HD:(k * groups + g + 1) * HD,
                    ] = (both[:, :HD] / both[:, HD:]).astype(jnp.bfloat16)
    for copy in copies:
        copy.wait()


def in_vmem(x):
    return pltpu.with_memory_space_constraint(x, VMEM)


def run_stage(small, query, offsets, blocks, carry, last, capacity):
    rows, columns = query.shape
    groups = H // KVH
    heads = columns // (groups * HD)
    cycle = small[3].shape[0]
    requests = small[1].shape[0]
    pieces = rows // PIECE
    first = carry is None
    parts = tuple(len(block) for block in blocks)
    flat = [in_vmem(ref) for block in blocks for ref in block]
    hbm, vmem = pl.BlockSpec(memory_space=HBM), pl.BlockSpec(memory_space=VMEM)
    small = tuple(pltpu.with_memory_space_constraint(x, HBM) for x in small)
    operands = [*small, query if first else in_vmem(query), *flat]
    specs = [hbm] * 4 + [hbm if first else vmem] + [vmem] * len(flat)
    unit = groups * PIECE
    max_shape = VMEM((heads, pieces, unit, HD), jnp.float32)
    acc_shape = VMEM((heads, pieces, unit, 2 * HD), jnp.float32)
    decode_shape = jax.ShapeDtypeStruct((capacity * cycle, heads * HD), jnp.bfloat16)
    alias = {}
    at = len(operands)
    if not first:
        operands += [in_vmem(carry[0]), in_vmem(carry[1]), *carry[2:]]
        specs += [vmem] * 2 + [hbm] * 2
    if last:
        out_shape = (jax.ShapeDtypeStruct((rows, columns), jnp.bfloat16), decode_shape, decode_shape)
        out_specs = (vmem, hbm, hbm)
        alias = {at + 2: 1, at + 3: 2}
    else:
        out_shape = (max_shape, acc_shape, decode_shape, decode_shape)
        out_specs = (vmem, vmem, hbm, hbm)
        if first:
            out_shape += (VMEM((rows, columns), jnp.bfloat16),)
            out_specs += (vmem,)
        else:
            alias = {at + j: j for j in range(4)}
    body = functools.partial(
        stage_kernel, offsets, parts, first, last, rows, heads, groups, requests, capacity
    )
    keys = 2 * rows * len(blocks)
    return pl.pallas_call(
        body,
        out_shape=out_shape,
        in_specs=specs,
        out_specs=out_specs,
        input_output_aliases=alias,
        scratch_shapes=[
            *[SMEM(x.shape, jnp.int32) for x in small[:3]],
            VMEM(small[3].shape, jnp.int32),
            VMEM((len(blocks), 2, capacity, heads * HD), jnp.bfloat16),
            pltpu.SemaphoreType.DMA((len(blocks), 2)),
            pltpu.SemaphoreType.DMA((5,)),
        ],
        compiler_params=pltpu.CompilerParams(vmem_limit_bytes=20 * 1024 * 1024),
        cost_estimate=pl.CostEstimate(
            flops=4 * rows * columns * keys, bytes_accessed=4 * 1024 * 1024, transcendentals=0
        ),
    )(*operands)


def pack_kernel(*refs):
    *inputs, out_ref, sems = refs
    rows = inputs[0].shape[0]
    copies = [
        pltpu.make_async_copy(ref, out_ref.at[j * rows:(j + 1) * rows], sems.at[j])
        for j, ref in enumerate(inputs)
    ]
    for copy in copies:
        copy.start()
    for copy in copies:
        copy.wait()


def pack(*arrays):
    rows, columns = arrays[0].shape
    return pl.pallas_call(
        pack_kernel,
        out_shape=VMEM((rows * len(arrays), columns), jnp.bfloat16),
        in_specs=[pl.BlockSpec(memory_space=HBM)] * len(arrays),
        out_specs=pl.BlockSpec(memory_space=VMEM),
        scratch_shapes=[pltpu.SemaphoreType.DMA((len(arrays),))],
        compiler_params=pltpu.CompilerParams(vmem_limit_bytes=4 * 1024 * 1024),
    )(*(pltpu.with_memory_space_constraint(x, HBM) for x in arrays))


def choose_kernel(pairs, *refs):
    inputs, outputs = refs[:2 * pairs], refs[2 * pairs:]
    place = lax.axis_index("blk") // 2
    outer = (place == 0) | (place == 3)
    for j in range(pairs):
        @pl.when(outer)
        def _():
            outputs[j][...] = inputs[2 * j][...]

        @pl.when(jnp.logical_not(outer))
        def _():
            outputs[j][...] = inputs[2 * j + 1][...]


def choose(at_ends, between):
    vmem = pl.BlockSpec(memory_space=VMEM)
    return pl.pallas_call(
        functools.partial(choose_kernel, 1),
        out_shape=VMEM(at_ends.shape, at_ends.dtype),
        in_specs=[vmem] * 2,
        out_specs=vmem,
        compiler_params=pltpu.CompilerParams(vmem_limit_bytes=8 * 1024 * 1024),
    )(in_vmem(at_ends), in_vmem(between))


def together(values, *after):
    return lax.optimization_barrier(tuple(values) + after)[: len(values)]


def cycle_of_eight(
    queries, new_keys, new_values, prefix_keys, prefix_values, span_lens, prefix_lens, placement, decode_dest
):
    cycle = lax.axis_size("blk")
    rows = queries.shape[0]
    capacity = 2 * rows // cycle

    def moves(table):
        return [(2 * a + y, 2 * b + y) for a, b in table.items() for y in range(2)]

    swap = [(i, i ^ 1) for i in range(cycle)]
    near = moves({0: 1, 1: 0, 2: 3, 3: 2})
    middle = moves({1: 2, 2: 1})
    ends = moves({0: 3, 3: 0})
    skip = moves({0: 2, 3: 1, 2: 3, 1: 0})
    send = lambda x, table: lax.ppermute(x, "blk", table)

    small = (placement, span_lens, prefix_lens, decode_dest.reshape(cycle, rows))
    own = pack(prefix_keys, prefix_values, new_keys, new_values)
    half = own.shape[0] // 2

    a = send(own, near)
    y_own = send(own, swap)
    b_inner = send(own, middle)
    *carry, query = run_stage(small, queries, (0,), [[own]], None, False, capacity)

    own_2, a_2, *carry = together((own, a, *carry), y_own)
    b_outer = send(own_2, ends)
    y_a = send(a_2, swap)
    carry = run_stage(small, query, (2, 1), [[a_2], [y_own]], carry, False, capacity)

    b = choose(b_outer, b_inner)
    (skip_from,) = together((choose(own_2, b_inner),), b_outer, *carry[:1])
    c = send(skip_from, skip)
    b, *carry = together((b, *carry), y_a)
    y_b = send(b, swap)
    carry = run_stage(small, query, (6, 3), [[b], [y_a]], carry, False, capacity)

    c_low, *carry = together((c[:half], *carry), y_b)
    y_c_low = send(c_low, swap)
    (y_b_high,) = together((y_b[half:],), c, carry[0])
    y_c_high = send(y_b_high, near)
    carry = run_stage(small, query, (4, 7), [[c], [y_b]], carry, False, capacity)
    return tuple(run_stage(small, query, (5,), [[y_c_low, y_c_high]], carry, True, capacity))


masked_score = -1e30


def request_of(index, lens):
    ends = jnp.cumsum(lens)
    return jnp.sum((index[:, None] >= ends[None, :]).astype(jnp.int32), axis=1)


def block_rows_for(length):
    chosen = 512
    while length % chosen:
        chosen = chosen // 2
    return chosen


def attend(carried, query_groups, query_req, query_tok, keys, values, key_req, key_tok):
    length = keys.shape[0]
    chosen = block_rows_for(length)
    blocks = length // chosen
    heads_here = query_groups.shape[1]
    score_scale = 1.0 / math.sqrt(HD)
    key_blocks = keys.reshape(blocks, chosen, heads_here, HD)
    value_blocks = values.reshape(blocks, chosen, heads_here, HD)
    req_blocks = key_req.reshape(blocks, chosen)
    tok_blocks = key_tok.reshape(blocks, chosen)

    def one_block(inner, items):
        running_max, running_sum, numerator = inner
        key_part, value_part, req_part, tok_part = items
        visible = (req_part[None, :] == query_req[:, None]) & (
            tok_part[None, :] <= query_tok[:, None]
        )
        scores = (
            jnp.einsum("tkgd,nkd->kgtn", query_groups, key_part, preferred_element_type=jnp.float32)
            * score_scale
        )
        scores = jnp.where(visible, scores, masked_score)
        new_max = jnp.maximum(running_max, jnp.max(scores, axis=-1))
        rescale = jnp.exp(running_max - new_max)
        weights = jnp.where(visible, jnp.exp(scores - new_max[..., None]), 0.0)
        running_sum = running_sum * rescale + jnp.sum(weights, axis=-1)
        numerator = numerator * rescale[..., None] + jnp.einsum(
            "kgtn,nkd->kgtd",
            weights.astype(jnp.bfloat16),
            value_part,
            preferred_element_type=jnp.float32,
        )
        return ((new_max, running_sum, numerator), None)

    result, ignored = lax.scan(
        one_block, carried, (key_blocks, value_blocks, req_blocks, tok_blocks)
    )
    return result


def maybe_attend(
    carried, query_groups, query_req, query_tok, summary, keys, values, key_req, key_tok
):
    query_has, query_last = summary
    request_ids = jnp.arange(query_has.shape[0], dtype=jnp.int32)
    matches = key_req[:, None] == request_ids[None, :]
    wanted = jnp.any(matches & query_has[None, :], axis=1)
    latest = jnp.max(jnp.where(matches, query_last[None, :], -2), axis=1)
    touched = jnp.any(wanted & (key_tok <= latest))
    return lax.cond(
        touched,
        lambda inner: attend(
            inner, query_groups, query_req, query_tok, keys, values, key_req, key_tok
        ),
        lambda inner: inner,
        carried,
    )


def any_cycle(
    queries,
    new_keys,
    new_values,
    prefix_keys,
    prefix_values,
    span_lens,
    prefix_lens,
    placement,
    decode_dest,
):
    cycle_size = lax.axis_size("blk")
    my_index = lax.axis_index("blk")
    rows_here = queries.shape[0]
    kv_cols = new_keys.shape[1]
    heads_here = kv_cols // HD
    groups = H // KVH
    query_groups = queries.reshape(rows_here, heads_here, groups, HD)
    query_tok = lax.dynamic_slice_in_dim(placement, my_index * rows_here, rows_here)
    query_req = request_of(query_tok, span_lens)
    token_req = request_of(placement, span_lens)
    prefix_total = prefix_keys.shape[0] * cycle_size
    prefix_req = request_of(jnp.arange(prefix_total, dtype=jnp.int32), prefix_lens)
    request_ids = jnp.arange(span_lens.shape[0], dtype=jnp.int32)
    member = query_req[:, None] == request_ids[None, :]
    summary = (jnp.any(member, axis=0), jnp.max(jnp.where(member, query_tok[:, None], -1), axis=0))
    initial = (
        jnp.full((heads_here, groups, rows_here), masked_score, jnp.float32),
        jnp.zeros((heads_here, groups, rows_here), jnp.float32),
        jnp.zeros((heads_here, groups, rows_here, HD), jnp.float32),
    )
    piece_keys = lax.all_gather(prefix_keys, "blk", axis=0, tiled=True)
    piece_values = lax.all_gather(prefix_values, "blk", axis=0, tiled=True)
    length = piece_keys.shape[0]
    key_req = prefix_req
    key_tok = jnp.full((length,), -1, jnp.int32)
    carried = maybe_attend(
        initial,
        query_groups,
        query_req,
        query_tok,
        summary,
        piece_keys,
        piece_values,
        key_req,
        key_tok,
    )
    destination = decode_dest[:, 0]
    capacity = 2 * rows_here // cycle_size
    piece_keys = lax.all_gather(new_keys, "blk", axis=0, tiled=True)
    piece_values = lax.all_gather(new_values, "blk", axis=0, tiled=True)
    key_req = token_req
    key_tok = placement
    carried = maybe_attend(
        carried,
        query_groups,
        query_req,
        query_tok,
        summary,
        piece_keys,
        piece_values,
        key_req,
        key_tok,
    )
    local_dest = lax.dynamic_slice_in_dim(destination, my_index * rows_here, rows_here)
    one_hot = (local_dest[:, None] == jnp.arange(cycle_size, dtype=jnp.int32)[None, :]).astype(
        jnp.int32
    )
    slot_rank = jnp.sum(jnp.cumsum(one_hot, axis=0) * one_hot, axis=1) - 1
    target = local_dest * capacity + slot_rank
    selector = (
        jnp.arange(cycle_size * capacity, dtype=jnp.int32)[:, None] == target[None, :]
    ).astype(jnp.bfloat16)
    stacked = jnp.concatenate([new_keys, new_values], axis=1)
    outgoing = jnp.dot(selector, stacked, preferred_element_type=jnp.float32).astype(jnp.bfloat16)
    moved = lax.all_to_all(outgoing, "blk", split_axis=0, concat_axis=0, tiled=True)
    running_max, running_sum, numerator = carried
    attended = (
        (numerator / running_sum[..., None])
        .transpose(2, 0, 1, 3)
        .reshape(rows_here, heads_here * groups * HD)
        .astype(jnp.bfloat16)
    )
    return (attended, moved[:, :kv_cols], moved[:, kv_cols:])


def solution(mesh):
    rows = P(("groups", "blk"), "tensor")
    return jax.shard_map(
        cycle_of_eight if mesh.shape["blk"] == 8 else any_cycle,
        mesh=mesh,
        in_specs=(rows,) * 5 + (P("groups"),) * 3 + (P("groups", None),),
        out_specs=(rows,) * 3,
        check_vma=False,
    )
```

```python
import functools
import math

import jax
import jax.numpy as jnp
from jax import lax
from jax.experimental import pallas as pl
from jax.experimental.pallas import tpu as pltpu
from jax.sharding import PartitionSpec as P

H = 64
KVH = 8
HD = 128
PIECE = 64
LARGE_NEGATIVE = -1e30

VMEM = pltpu.VMEM
SMEM = pltpu.SMEM
HBM = pltpu.HBM


def dot_nt(a, b):
    return lax.dot_general(a, b, (((1,), (1,)), ((), ())), preferred_element_type=jnp.float32)


def dot_nn(a, b):
    return lax.dot_general(a, b, (((1,), (0,)), ((), ())), preferred_element_type=jnp.float32)


def stage_kernel(offsets, parts, first, last, rows, heads, groups, requests, capacity, *refs):
    refs = list(refs)
    small_in, query_ref = refs[:4], refs[4]
    refs = refs[5:]
    blocks = []
    for count in parts:
        blocks.append(refs[:count])
        refs = refs[count:]
    if not first:
        max_in, acc_in = refs[:2]
        refs = refs[4:]
    if last:
        att_ref, dkey_ref, dval_ref = refs[:3]
        refs = refs[3:]
        max_ref, acc_ref = max_in, acc_in
    else:
        max_ref, acc_ref, dkey_ref, dval_ref = refs[:4]
        refs = refs[4:]
    if first:
        query_in, query_ref = query_ref, refs[0]
        refs = refs[1:]
    place_ref, span_ref, plen_ref, dest_ref, picked_ref, sems, small_sems = refs
    small = [
        pltpu.make_async_copy(source, target, small_sems.at[j])
        for j, (source, target) in enumerate(
            zip(small_in, (place_ref, span_ref, plen_ref, dest_ref))
        )
    ]
    if first:
        small.append(pltpu.make_async_copy(query_in, query_ref, small_sems.at[4]))
    for copy in small:
        copy.start()
    for copy in small:
        copy.wait()
    me = lax.axis_index("blk")
    pieces = rows // PIECE
    unit = groups * PIECE
    factor = math.log2(math.e) / math.sqrt(HD)

    def bounds(token):
        low = jnp.zeros_like(token)
        pre_low = jnp.zeros_like(token)
        pre_high = jnp.zeros_like(token) + plen_ref[0]
        end = jnp.int32(0)
        for r in range(requests - 1):
            end = end + span_ref[r]
            past = token >= end
            low = low + jnp.where(past, span_ref[r], 0)
            pre_low = pre_low + jnp.where(past, plen_ref[r], 0)
            pre_high = pre_high + jnp.where(past, plen_ref[r + 1], 0)
        return low, pre_low, pre_high

    def part_of(block, which, start, size):
        if len(block) == 1:
            return block[0][which * rows:(which + 1) * rows, pl.ds(start, size)]
        half, inner = divmod(which, 2)
        return block[half][inner * rows:(inner + 1) * rows, pl.ds(start, size)]

    copies = []
    for n, (offset, block) in enumerate(zip(offsets, blocks)):
        index = me ^ offset
        for piece in range(pieces):
            base = place_ref[me * rows + piece * PIECE]
            low0, pre0, unused = bounds(base)
            unused, unused2, pre1 = bounds(base + (PIECE - 1))
            seen = (pre0 < (index + 1) * rows) & (pre1 > index * rows)
            for other in range(pieces):
                there = place_ref[index * rows + other * PIECE]
                seen = seen | ((there <= base) & (there + (PIECE - 1) >= low0))

            def work(piece=piece, base=base, block=block, index=index, n=n):
                token = base + lax.broadcasted_iota(jnp.int32, (PIECE, 1), 0)
                low, pre_low, pre_high = bounds(token)
                column = lax.broadcasted_iota(jnp.int32, (PIECE, rows), 1)
                position = column + index * rows
                pre_seen = (position >= pre_low) & (position < pre_high)
                key_token = jnp.zeros((PIECE, rows), jnp.int32)
                for other in range(pieces):
                    there = place_ref[index * rows + other * PIECE] - other * PIECE
                    key_token = jnp.where(column >= other * PIECE, column + there, key_token)
                new_seen = (key_token >= low) & (key_token <= token)
                bias = jnp.concatenate(
                    [
                        jnp.where(pre_seen, 0.0, LARGE_NEGATIVE),
                        jnp.where(new_seen, 0.0, LARGE_NEGATIVE),
                    ],
                    axis=1,
                ).astype(jnp.float32)
                step = 4
                for k in range(heads):
                    keys = jnp.concatenate(
                        [part_of(block, 0, k * HD, HD), part_of(block, 2, k * HD, HD)], axis=0
                    )
                    values = jnp.concatenate(
                        [part_of(block, 1, k * HD, HD), part_of(block, 3, k * HD, HD)], axis=0
                    )
                    values = jnp.concatenate([values, jnp.ones_like(values)], axis=1)
                    for g in range(0, groups, step):
                        query = jnp.concatenate(
                            [
                                query_ref[
                                    piece * PIECE:(piece + 1) * PIECE,
                                    (k * groups + g + j) * HD:(k * groups + g + j + 1) * HD,
                                ]
                                for j in range(step)
                            ],
                            axis=0,
                        )
                        scores = dot_nt(query, keys) * factor
                        scores = scores.reshape(step, PIECE, 2 * rows) + bias[None]
                        scores = scores.reshape(step * PIECE, 2 * rows)
                        at = slice(g * PIECE, (g + step) * PIECE)
                        here = jnp.max(scores, axis=1, keepdims=True)
                        if first and n == 0:
                            new_max = jnp.broadcast_to(here, (step * PIECE, HD))
                        else:
                            source_max, source_acc = (
                                (max_in, acc_in) if n == 0 and not first else (max_ref, acc_ref)
                            )
                            old_max = source_max[k, piece, at, :]
                            new_max = jnp.maximum(old_max, here)
                        weights = jnp.exp2(scores - jnp.concatenate([new_max, new_max], axis=1))
                        added = dot_nn(weights.astype(jnp.bfloat16), values)
                        if not (first and n == 0):
                            rescale = jnp.exp2(old_max - new_max)
                            rescale = jnp.concatenate([rescale, rescale], axis=1)
                            added = source_acc[k, piece, at, :] * rescale + added
                        acc_ref[k, piece, at, :] = added
                        max_ref[k, piece, at, :] = new_max

            if first and n == 0:
                work()
            else:
                pl.when(seen)(work)
        mine = jnp.where(dest_ref[pl.ds(index, 1), :] == me, 1.0, 0.0)
        lane = lax.broadcasted_iota(jnp.int32, (rows, rows), 0)
        lane2 = lax.broadcasted_iota(jnp.int32, (rows, rows), 1)
        earlier = jnp.where(lane < lane2, 1.0, 0.0).astype(jnp.bfloat16)
        mine = jnp.broadcast_to(mine, (capacity, rows))
        rank = dot_nn(mine.astype(jnp.bfloat16), earlier)
        slot = lax.broadcasted_iota(jnp.int32, (capacity, rows), 0).astype(jnp.float32)
        choose = jnp.where((rank == slot) & (mine > 0.5), 1.0, 0.0).astype(jnp.bfloat16)
        for which, out_ref in ((2, dkey_ref), (3, dval_ref)):
            picked_ref[n, which - 2] = dot_nn(choose, part_of(block, which, 0, heads * HD)).astype(
                jnp.bfloat16
            )
            copy = pltpu.make_async_copy(
                picked_ref.at[n, which - 2],
                out_ref.at[pl.ds(pl.multiple_of(index * capacity, capacity), capacity)],
                sems.at[n, which - 2],
            )
            copy.start()
            copies.append(copy)
    if last:
        for piece in range(pieces):
            for k in range(heads):
                for g in range(groups):
                    both = acc_ref[k, piece, g * PIECE:(g + 1) * PIECE, :]
                    att_ref[
                        piece * PIECE:(piece + 1) * PIECE,
                        (k * groups + g) * HD:(k * groups + g + 1) * HD,
                    ] = (both[:, :HD] / both[:, HD:]).astype(jnp.bfloat16)
    for copy in copies:
        copy.wait()


def in_vmem(x):
    return pltpu.with_memory_space_constraint(x, VMEM)


def run_stage(small, query, offsets, blocks, carry, last, capacity):
    rows, columns = query.shape
    groups = H // KVH
    heads = columns // (groups * HD)
    cycle = small[3].shape[0]
    requests = small[1].shape[0]
    pieces = rows // PIECE
    first = carry is None
    parts = tuple(len(block) for block in blocks)
    flat = [in_vmem(ref) for block in blocks for ref in block]
    hbm, vmem = pl.BlockSpec(memory_space=HBM), pl.BlockSpec(memory_space=VMEM)
    small = tuple(pltpu.with_memory_space_constraint(x, HBM) for x in small)
    operands = [*small, query if first else in_vmem(query), *flat]
    specs = [hbm] * 4 + [hbm if first else vmem] + [vmem] * len(flat)
    unit = groups * PIECE
    max_shape = VMEM((heads, pieces, unit, HD), jnp.float32)
    acc_shape = VMEM((heads, pieces, unit, 2 * HD), jnp.float32)
    decode_shape = jax.ShapeDtypeStruct((capacity * cycle, heads * HD), jnp.bfloat16)
    alias = {}
    at = len(operands)
    if not first:
        operands += [in_vmem(carry[0]), in_vmem(carry[1]), *carry[2:]]
        specs += [vmem] * 2 + [hbm] * 2
    if last:
        out_shape = (jax.ShapeDtypeStruct((rows, columns), jnp.bfloat16), decode_shape, decode_shape)
        out_specs = (vmem, hbm, hbm)
        alias = {at + 2: 1, at + 3: 2}
    else:
        out_shape = (max_shape, acc_shape, decode_shape, decode_shape)
        out_specs = (vmem, vmem, hbm, hbm)
        if first:
            out_shape += (VMEM((rows, columns), jnp.bfloat16),)
            out_specs += (vmem,)
        else:
            alias = {at + j: j for j in range(4)}
    body = functools.partial(
        stage_kernel, offsets, parts, first, last, rows, heads, groups, requests, capacity
    )
    keys = 2 * rows * len(blocks)
    return pl.pallas_call(
        body,
        out_shape=out_shape,
        in_specs=specs,
        out_specs=out_specs,
        input_output_aliases=alias,
        scratch_shapes=[
            *[SMEM(x.shape, jnp.int32) for x in small[:3]],
            VMEM(small[3].shape, jnp.int32),
            VMEM((len(blocks), 2, capacity, heads * HD), jnp.bfloat16),
            pltpu.SemaphoreType.DMA((len(blocks), 2)),
            pltpu.SemaphoreType.DMA((5,)),
        ],
        compiler_params=pltpu.CompilerParams(vmem_limit_bytes=20 * 1024 * 1024),
        cost_estimate=pl.CostEstimate(
            flops=4 * rows * columns * keys, bytes_accessed=4 * 1024 * 1024, transcendentals=0
        ),
    )(*operands)


def pack_kernel(*refs):
    *inputs, out_ref, sems = refs
    rows = inputs[0].shape[0]
    copies = [
        pltpu.make_async_copy(ref, out_ref.at[j * rows:(j + 1) * rows], sems.at[j])
        for j, ref in enumerate(inputs)
    ]
    for copy in copies:
        copy.start()
    for copy in copies:
        copy.wait()


def pack(*arrays):
    rows, columns = arrays[0].shape
    return pl.pallas_call(
        pack_kernel,
        out_shape=VMEM((rows * len(arrays), columns), jnp.bfloat16),
        in_specs=[pl.BlockSpec(memory_space=HBM)] * len(arrays),
        out_specs=pl.BlockSpec(memory_space=VMEM),
        scratch_shapes=[pltpu.SemaphoreType.DMA((len(arrays),))],
        compiler_params=pltpu.CompilerParams(vmem_limit_bytes=4 * 1024 * 1024),
    )(*(pltpu.with_memory_space_constraint(x, HBM) for x in arrays))


def choose_kernel(at_ends, between, *refs):
    out_ref = refs[-1]
    place = lax.axis_index("blk") // 2
    outer = (place == 0) | (place == 3)

    @pl.when(outer)
    def _():
        out_ref[...] = at_ends[...]

    @pl.when(jnp.logical_not(outer))
    def _():
        out_ref[...] = between[...]


def choose(at_ends, between, *after):
    vmem = pl.BlockSpec(memory_space=VMEM)
    return pl.pallas_call(
        choose_kernel,
        out_shape=VMEM(at_ends.shape, at_ends.dtype),
        in_specs=[vmem] * (2 + len(after)),
        out_specs=vmem,
        compiler_params=pltpu.CompilerParams(vmem_limit_bytes=8 * 1024 * 1024),
    )(in_vmem(at_ends), in_vmem(between), *(in_vmem(x) for x in after))


def half_kernel(which, in_ref, *refs):
    out_ref = refs[-1]
    rows = out_ref.shape[0]
    out_ref[...] = in_ref[which * rows:(which + 1) * rows]


def half_of(x, which, *after):
    vmem = pl.BlockSpec(memory_space=VMEM)
    return pl.pallas_call(
        functools.partial(half_kernel, which),
        out_shape=VMEM((x.shape[0] // 2, x.shape[1]), x.dtype),
        in_specs=[vmem] * (1 + len(after)),
        out_specs=vmem,
        compiler_params=pltpu.CompilerParams(vmem_limit_bytes=8 * 1024 * 1024),
    )(in_vmem(x), *(in_vmem(y) for y in after))


def together(values, *after):
    return lax.optimization_barrier(tuple(values) + after)[: len(values)]


def cycle_of_eight(
    queries, new_keys, new_values, prefix_keys, prefix_values, span_lens, prefix_lens, placement, decode_dest
):
    cycle = lax.axis_size("blk")
    rows = queries.shape[0]
    capacity = 2 * rows // cycle

    def moves(table):
        return [(2 * a + y, 2 * b + y) for a, b in table.items() for y in range(2)]

    swap = [(i, i ^ 1) for i in range(cycle)]
    near = moves({0: 1, 1: 0, 2: 3, 3: 2})
    middle = moves({1: 2, 2: 1})
    ends = moves({0: 3, 3: 0})
    skip = moves({0: 2, 3: 1, 2: 3, 1: 0})
    send = lambda x, table: lax.ppermute(x, "blk", table)

    small = (placement, span_lens, prefix_lens, decode_dest.reshape(cycle, rows))
    own = pack(prefix_keys, prefix_values, new_keys, new_values)
    half = own.shape[0] // 2

    a = send(own, near)
    y_own = send(own, swap)
    b_inner = send(own, middle)
    *carry, query = run_stage(small, queries, (0,), [[own]], None, False, capacity)

    skip_from = choose(own, b_inner, y_own)
    a_2, *carry = together((a, *carry))
    y_a = send(a_2, swap)
    own_2, *carry = together((own, *carry), skip_from)
    b_outer = send(own_2, ends)
    carry = run_stage(small, query, (2, 1), [[a_2], [y_own]], carry, False, capacity)

    b = choose(b_outer, choose(b_inner, b_inner, y_a))
    b, *carry = together((b, *carry))
    y_b = send(b, swap)
    skip_from, *carry = together((skip_from, *carry), b, y_a)
    c = send(skip_from, skip)
    carry = run_stage(small, query, (6, 3), [[b], [y_a]], carry, False, capacity)

    y_b_high, *carry = together((half_of(y_b, 1), *carry))
    y_c_high = send(y_b_high, near)
    c_low, *carry = together((half_of(c, 0, y_b_high), *carry))
    y_c_low = send(c_low, swap)
    carry = run_stage(small, query, (4, 7), [[c], [y_b]], carry, False, capacity)
    return tuple(run_stage(small, query, (5,), [[y_c_low, y_c_high]], carry, True, capacity))


masked_score = -1e30


def request_of(index, lens):
    ends = jnp.cumsum(lens)
    return jnp.sum((index[:, None] >= ends[None, :]).astype(jnp.int32), axis=1)


def block_rows_for(length):
    chosen = 512
    while length % chosen:
        chosen = chosen // 2
    return chosen


def attend(carried, query_groups, query_req, query_tok, keys, values, key_req, key_tok):
    length = keys.shape[0]
    chosen = block_rows_for(length)
    blocks = length // chosen
    heads_here = query_groups.shape[1]
    score_scale = 1.0 / math.sqrt(HD)
    key_blocks = keys.reshape(blocks, chosen, heads_here, HD)
    value_blocks = values.reshape(blocks, chosen, heads_here, HD)
    req_blocks = key_req.reshape(blocks, chosen)
    tok_blocks = key_tok.reshape(blocks, chosen)

    def one_block(inner, items):
        running_max, running_sum, numerator = inner
        key_part, value_part, req_part, tok_part = items
        visible = (req_part[None, :] == query_req[:, None]) & (
            tok_part[None, :] <= query_tok[:, None]
        )
        scores = (
            jnp.einsum("tkgd,nkd->kgtn", query_groups, key_part, preferred_element_type=jnp.float32)
            * score_scale
        )
        scores = jnp.where(visible, scores, masked_score)
        new_max = jnp.maximum(running_max, jnp.max(scores, axis=-1))
        rescale = jnp.exp(running_max - new_max)
        weights = jnp.where(visible, jnp.exp(scores - new_max[..., None]), 0.0)
        running_sum = running_sum * rescale + jnp.sum(weights, axis=-1)
        numerator = numerator * rescale[..., None] + jnp.einsum(
            "kgtn,nkd->kgtd",
            weights.astype(jnp.bfloat16),
            value_part,
            preferred_element_type=jnp.float32,
        )
        return ((new_max, running_sum, numerator), None)

    result, ignored = lax.scan(
        one_block, carried, (key_blocks, value_blocks, req_blocks, tok_blocks)
    )
    return result


def maybe_attend(
    carried, query_groups, query_req, query_tok, summary, keys, values, key_req, key_tok
):
    query_has, query_last = summary
    request_ids = jnp.arange(query_has.shape[0], dtype=jnp.int32)
    matches = key_req[:, None] == request_ids[None, :]
    wanted = jnp.any(matches & query_has[None, :], axis=1)
    latest = jnp.max(jnp.where(matches, query_last[None, :], -2), axis=1)
    touched = jnp.any(wanted & (key_tok <= latest))
    return lax.cond(
        touched,
        lambda inner: attend(
            inner, query_groups, query_req, query_tok, keys, values, key_req, key_tok
        ),
        lambda inner: inner,
        carried,
    )


def any_cycle(
    queries,
    new_keys,
    new_values,
    prefix_keys,
    prefix_values,
    span_lens,
    prefix_lens,
    placement,
    decode_dest,
):
    cycle_size = lax.axis_size("blk")
    my_index = lax.axis_index("blk")
    rows_here = queries.shape[0]
    kv_cols = new_keys.shape[1]
    heads_here = kv_cols // HD
    groups = H // KVH
    query_groups = queries.reshape(rows_here, heads_here, groups, HD)
    query_tok = lax.dynamic_slice_in_dim(placement, my_index * rows_here, rows_here)
    query_req = request_of(query_tok, span_lens)
    token_req = request_of(placement, span_lens)
    prefix_total = prefix_keys.shape[0] * cycle_size
    prefix_req = request_of(jnp.arange(prefix_total, dtype=jnp.int32), prefix_lens)
    request_ids = jnp.arange(span_lens.shape[0], dtype=jnp.int32)
    member = query_req[:, None] == request_ids[None, :]
    summary = (jnp.any(member, axis=0), jnp.max(jnp.where(member, query_tok[:, None], -1), axis=0))
    initial = (
        jnp.full((heads_here, groups, rows_here), masked_score, jnp.float32),
        jnp.zeros((heads_here, groups, rows_here), jnp.float32),
        jnp.zeros((heads_here, groups, rows_here, HD), jnp.float32),
    )
    piece_keys = lax.all_gather(prefix_keys, "blk", axis=0, tiled=True)
    piece_values = lax.all_gather(prefix_values, "blk", axis=0, tiled=True)
    length = piece_keys.shape[0]
    key_req = prefix_req
    key_tok = jnp.full((length,), -1, jnp.int32)
    carried = maybe_attend(
        initial,
        query_groups,
        query_req,
        query_tok,
        summary,
        piece_keys,
        piece_values,
        key_req,
        key_tok,
    )
    destination = decode_dest[:, 0]
    capacity = 2 * rows_here // cycle_size
    piece_keys = lax.all_gather(new_keys, "blk", axis=0, tiled=True)
    piece_values = lax.all_gather(new_values, "blk", axis=0, tiled=True)
    key_req = token_req
    key_tok = placement
    carried = maybe_attend(
        carried,
        query_groups,
        query_req,
        query_tok,
        summary,
        piece_keys,
        piece_values,
        key_req,
        key_tok,
    )
    local_dest = lax.dynamic_slice_in_dim(destination, my_index * rows_here, rows_here)
    one_hot = (local_dest[:, None] == jnp.arange(cycle_size, dtype=jnp.int32)[None, :]).astype(
        jnp.int32
    )
    slot_rank = jnp.sum(jnp.cumsum(one_hot, axis=0) * one_hot, axis=1) - 1
    target = local_dest * capacity + slot_rank
    selector = (
        jnp.arange(cycle_size * capacity, dtype=jnp.int32)[:, None] == target[None, :]
    ).astype(jnp.bfloat16)
    stacked = jnp.concatenate([new_keys, new_values], axis=1)
    outgoing = jnp.dot(selector, stacked, preferred_element_type=jnp.float32).astype(jnp.bfloat16)
    moved = lax.all_to_all(outgoing, "blk", split_axis=0, concat_axis=0, tiled=True)
    running_max, running_sum, numerator = carried
    attended = (
        (numerator / running_sum[..., None])
        .transpose(2, 0, 1, 3)
        .reshape(rows_here, heads_here * groups * HD)
        .astype(jnp.bfloat16)
    )
    return (attended, moved[:, :kv_cols], moved[:, kv_cols:])


def solution(mesh):
    rows = P(("groups", "blk"), "tensor")
    return jax.shard_map(
        cycle_of_eight if mesh.shape["blk"] == 8 else any_cycle,
        mesh=mesh,
        in_specs=(rows,) * 5 + (P("groups"),) * 3 + (P("groups", None),),
        out_specs=(rows,) * 3,
        check_vma=False,
    )
```

```python
import functools
import math

import jax
import jax.numpy as jnp
from jax import lax
from jax.experimental import pallas as pl
from jax.experimental.pallas import tpu as pltpu
from jax.sharding import PartitionSpec as P

H = 64
KVH = 8
HD = 128
PIECE = 64
LARGE_NEGATIVE = -1e30

VMEM = pltpu.VMEM
SMEM = pltpu.SMEM
HBM = pltpu.HBM


def dot_nt(a, b):
    return lax.dot_general(a, b, (((1,), (1,)), ((), ())), preferred_element_type=jnp.float32)


def dot_nn(a, b):
    return lax.dot_general(a, b, (((1,), (0,)), ((), ())), preferred_element_type=jnp.float32)


def part_of(block, which, rows, start, size):
    if len(block) == 1:
        return block[0][which * rows:(which + 1) * rows, start:start + size]
    half, inner = divmod(which, 2)
    return block[half][inner * rows:(inner + 1) * rows, start:start + size]


def add_blocks(blocks, biases, query_ref, before, after, heads, groups, store):
    rows = query_ref.shape[0]
    factor = math.log2(math.e) / math.sqrt(HD)
    step = 2
    for k in range(heads):
        keys, values = [], []
        for block in blocks:
            keys.append(
                jnp.concatenate(
                    [part_of(block, j, rows, k * HD, HD) for j in (0, 2)], axis=0
                )
            )
            value = jnp.concatenate(
                [part_of(block, j, rows, k * HD, HD) for j in (1, 3)], axis=0
            )
            values.append(jnp.concatenate([value, jnp.ones_like(value)], axis=1))
        for g in range(0, groups, step):
            query = jnp.concatenate(
                [
                    query_ref[:, (k * groups + g + j) * HD:(k * groups + g + j + 1) * HD]
                    for j in range(step)
                ],
                axis=0,
            )
            at = slice(g * rows, (g + step) * rows)
            scores = []
            for key, bias in zip(keys, biases):
                score = (dot_nt(query, key) * factor).reshape(step, rows, 2 * rows) + bias[...][None]
                scores.append(score.reshape(step * rows, 2 * rows))
            largest = functools.reduce(jnp.maximum, scores)
            new_max = jnp.broadcast_to(
                jnp.max(largest, axis=1, keepdims=True), (step * rows, HD)
            )
            if before is not None:
                old_max = before[0][k, at, :]
                new_max = jnp.maximum(old_max, new_max)
            both_max = jnp.concatenate([new_max, new_max], axis=1)
            added = None
            for score, value in zip(scores, values):
                weights = jnp.exp2(score - both_max).astype(jnp.bfloat16)
                term = dot_nn(weights, value)
                added = term if added is None else added + term
            if before is not None:
                rescale = jnp.exp2(old_max - new_max)
                rescale = jnp.concatenate([rescale, rescale], axis=1)
                added = before[1][k, at, :] * rescale + added
            if after is not None:
                after[0][k, at, :] = new_max
                after[1][k, at, :] = added
            else:
                for j in range(step):
                    both = added[j * rows:(j + 1) * rows]
                    store(k, g + j, both[:, :HD] / both[:, HD:])
        if after is None:
            store(k, None, None)


def pick_rows(offsets, blocks, choose_refs, out_refs, picked_ref, sems):
    me = lax.axis_index("blk")
    copies = []
    for n, (offset, block, choose_ref) in enumerate(zip(offsets, blocks, choose_refs)):
        capacity, rows = choose_ref.shape
        index = me ^ offset
        for which, out_ref in enumerate(out_refs):
            new = part_of(block, 2 + which, rows, 0, out_ref.shape[1])
            picked_ref[n, which] = dot_nn(choose_ref[...], new).astype(jnp.bfloat16)
            copy = pltpu.make_async_copy(
                picked_ref.at[n, which],
                out_ref.at[pl.ds(pl.multiple_of(index * capacity, capacity), capacity)],
                sems.at[n, which],
            )
            copy.start()
            copies.append(copy)
    return copies


def first_kernel(
    offsets, rows, heads, groups, requests, capacity,
    place_in, span_in, plen_in, dest_in, query_in, own_ref,
    max_ref, acc_ref, dkey_ref, dval_ref, query_ref, bias_ref, choose_ref,
    place_ref, span_ref, plen_ref, dest_ref, picked_ref, sems, small_sems,
):
    small = [
        pltpu.make_async_copy(source, target, small_sems.at[j])
        for j, (source, target) in enumerate(
            (
                (place_in, place_ref),
                (span_in, span_ref),
                (plen_in, plen_ref),
                (dest_in, dest_ref),
                (query_in, query_ref),
            )
        )
    ]
    for copy in small:
        copy.start()
    for copy in small:
        copy.wait()
    me = lax.axis_index("blk")
    pieces = rows // PIECE

    def bounds(token):
        low = jnp.zeros_like(token)
        pre_low = jnp.zeros_like(token)
        pre_high = jnp.zeros_like(token) + plen_ref[0]
        end = jnp.int32(0)
        for r in range(requests - 1):
            end = end + span_ref[r]
            past = token >= end
            low = low + jnp.where(past, span_ref[r], 0)
            pre_low = pre_low + jnp.where(past, plen_ref[r], 0)
            pre_high = pre_high + jnp.where(past, plen_ref[r + 1], 0)
        return low, pre_low, pre_high

    def tokens_of(index, shape, axis):
        place = lax.broadcasted_iota(jnp.int32, shape, axis)
        token = place
        for piece in range(pieces):
            start = place_ref[index * rows + piece * PIECE] - piece * PIECE
            token = jnp.where(place >= piece * PIECE, place + start, token)
        return token

    token = tokens_of(me, (rows, rows), 0)
    low, pre_low, pre_high = bounds(token)
    column = lax.broadcasted_iota(jnp.int32, (rows, rows), 1)
    earlier = jnp.where(lax.broadcasted_iota(jnp.int32, (rows, rows), 0) < column, 1.0, 0.0)
    earlier = earlier.astype(jnp.bfloat16)
    slot = lax.broadcasted_iota(jnp.int32, (capacity, rows), 0).astype(jnp.float32)
    for n, offset in enumerate(offsets):
        index = me ^ offset
        position = column + index * rows
        pre_seen = (position >= pre_low) & (position < pre_high)
        key_token = tokens_of(index, (rows, rows), 1)
        new_seen = (key_token >= low) & (key_token <= token)
        bias_ref[n, :, :rows] = jnp.where(pre_seen, 0.0, LARGE_NEGATIVE).astype(jnp.float32)
        bias_ref[n, :, rows:] = jnp.where(new_seen, 0.0, LARGE_NEGATIVE).astype(jnp.float32)
        mine = jnp.where(dest_ref[pl.ds(index, 1), :] == me, 1.0, 0.0)
        mine = jnp.broadcast_to(mine, (capacity, rows))
        rank = dot_nn(mine.astype(jnp.bfloat16), earlier)
        choose_ref[n] = jnp.where((rank == slot) & (mine > 0.5), 1.0, 0.0).astype(jnp.bfloat16)
    copies = pick_rows(
        (0,), [[own_ref]], [choose_ref.at[0]], (dkey_ref, dval_ref), picked_ref, sems
    )
    add_blocks(
        [[own_ref]], [bias_ref.at[0]], query_ref, None, (max_ref, acc_ref), heads, groups, None
    )
    for copy in copies:
        copy.wait()


def stage_kernel(order, offsets, parts, last, heads, groups, *refs):
    refs = list(refs)
    query_ref, bias_ref, choose_ref = refs[:3]
    refs = refs[3:]
    blocks = []
    for count in parts:
        blocks.append(refs[:count])
        refs = refs[count:]
    before = refs[:2]
    refs = refs[4:]
    if last:
        att_ref, dkey_ref, dval_ref, picked_ref, sems, att_vmem, att_sems = refs
        after = None
    else:
        max_ref, acc_ref, dkey_ref, dval_ref, picked_ref, sems = refs
        after = (max_ref, acc_ref)
    copies = pick_rows(
        offsets, blocks, [choose_ref.at[n] for n in order], (dkey_ref, dval_ref), picked_ref, sems
    )

    def store(k, g, result):
        if g is not None:
            att_vmem[:, (k * groups + g) * HD:(k * groups + g + 1) * HD] = result.astype(jnp.bfloat16)
            return
        columns = slice(k * groups * HD, (k + 1) * groups * HD)
        copy = pltpu.make_async_copy(
            att_vmem.at[:, columns], att_ref.at[:, columns], att_sems.at[k]
        )
        copy.start()
        copies.append(copy)

    add_blocks(
        blocks, [bias_ref.at[n] for n in order], query_ref, before, after, heads, groups, store
    )
    for copy in copies:
        copy.wait()


def in_vmem(x):
    return pltpu.with_memory_space_constraint(x, VMEM)


def shapes_of(rows, columns, cycle):
    groups = H // KVH
    heads = columns // (groups * HD)
    state = (
        VMEM((heads, groups * rows, HD), jnp.float32),
        VMEM((heads, groups * rows, 2 * HD), jnp.float32),
    )
    decode = jax.ShapeDtypeStruct((2 * rows, heads * HD), jnp.bfloat16)
    return groups, heads, state, (decode, decode)


def params(keys, rows, columns):
    return dict(
        compiler_params=pltpu.CompilerParams(vmem_limit_bytes=20 * 1024 * 1024),
        cost_estimate=pl.CostEstimate(
            flops=4 * rows * columns * keys, bytes_accessed=4 * 1024 * 1024, transcendentals=0
        ),
    )


def run_first(small, query, own, offsets, capacity):
    rows, columns = query.shape
    cycle = len(offsets)
    groups, heads, state, decode = shapes_of(rows, columns, cycle)
    hbm, vmem = pl.BlockSpec(memory_space=HBM), pl.BlockSpec(memory_space=VMEM)
    small = tuple(pltpu.with_memory_space_constraint(x, HBM) for x in small)
    *state, dkey, dval, query, bias, choose = pl.pallas_call(
        functools.partial(
            first_kernel, offsets, rows, heads, groups, small[1].shape[0], capacity
        ),
        out_shape=(
            *state,
            *decode,
            VMEM((rows, columns), jnp.bfloat16),
            VMEM((cycle, rows, 2 * rows), jnp.float32),
            VMEM((cycle, capacity, rows), jnp.bfloat16),
        ),
        in_specs=[hbm] * 5 + [vmem],
        out_specs=(vmem, vmem, hbm, hbm, vmem, vmem, vmem),
        scratch_shapes=[
            *[SMEM(x.shape, jnp.int32) for x in small[:3]],
            VMEM(small[3].shape, jnp.int32),
            VMEM((1, 2, capacity, heads * HD), jnp.bfloat16),
            pltpu.SemaphoreType.DMA((1, 2)),
            pltpu.SemaphoreType.DMA((5,)),
        ],
        **params(2 * rows, rows, columns),
    )(*small, pltpu.with_memory_space_constraint(query, HBM), in_vmem(own))
    return [*state, dkey, dval], (query, bias, choose)


def run_stage(common, order, offsets, blocks, carry, last):
    rows, columns = common[0].shape
    cycle, capacity, unused = common[2].shape
    groups, heads, state, decode = shapes_of(rows, columns, cycle)
    parts = tuple(len(block) for block in blocks)
    flat = [in_vmem(ref) for block in blocks for ref in block]
    hbm, vmem = pl.BlockSpec(memory_space=HBM), pl.BlockSpec(memory_space=VMEM)
    operands = [*(in_vmem(x) for x in common), *flat]
    at = len(operands)
    operands += [in_vmem(carry[0]), in_vmem(carry[1]), *carry[2:]]
    scratch = [
        VMEM((len(blocks), 2, capacity, heads * HD), jnp.bfloat16),
        pltpu.SemaphoreType.DMA((len(blocks), 2)),
    ]
    if last:
        out_shape = (jax.ShapeDtypeStruct((rows, columns), jnp.bfloat16), *decode)
        out_specs = (hbm, hbm, hbm)
        alias = {at + 2: 1, at + 3: 2}
        scratch += [VMEM((rows, columns), jnp.bfloat16), pltpu.SemaphoreType.DMA((heads,))]
    else:
        out_shape = (*state, *decode)
        out_specs = (vmem, vmem, hbm, hbm)
        alias = {at + j: j for j in range(4)}
    return pl.pallas_call(
        functools.partial(stage_kernel, order, offsets, parts, last, heads, groups),
        out_shape=out_shape,
        in_specs=[vmem] * (at + 2) + [hbm] * 2,
        out_specs=out_specs,
        input_output_aliases=alias,
        scratch_shapes=scratch,
        **params(2 * rows * len(blocks), rows, columns),
    )(*operands)


def pack_kernel(*refs):
    *inputs, out_ref, sems = refs
    rows = inputs[0].shape[0]
    copies = [
        pltpu.make_async_copy(ref, out_ref.at[j * rows:(j + 1) * rows], sems.at[j])
        for j, ref in enumerate(inputs)
    ]
    for copy in copies:
        copy.start()
    for copy in copies:
        copy.wait()


def pack(*arrays):
    rows, columns = arrays[0].shape
    return pl.pallas_call(
        pack_kernel,
        out_shape=VMEM((rows * len(arrays), columns), jnp.bfloat16),
        in_specs=[pl.BlockSpec(memory_space=HBM)] * len(arrays),
        out_specs=pl.BlockSpec(memory_space=VMEM),
        scratch_shapes=[pltpu.SemaphoreType.DMA((len(arrays),))],
        compiler_params=pltpu.CompilerParams(vmem_limit_bytes=4 * 1024 * 1024),
    )(*(pltpu.with_memory_space_constraint(x, HBM) for x in arrays))


def choose_kernel(at_ends, between, *refs):
    out_ref = refs[-1]
    place = lax.axis_index("blk") // 2
    outer = (place == 0) | (place == 3)

    @pl.when(outer)
    def _():
        out_ref[...] = at_ends[...]

    @pl.when(jnp.logical_not(outer))
    def _():
        out_ref[...] = between[...]


def choose(at_ends, between, *after):
    vmem = pl.BlockSpec(memory_space=VMEM)
    return pl.pallas_call(
        choose_kernel,
        out_shape=VMEM(at_ends.shape, at_ends.dtype),
        in_specs=[vmem] * (2 + len(after)),
        out_specs=vmem,
        compiler_params=pltpu.CompilerParams(vmem_limit_bytes=8 * 1024 * 1024),
    )(in_vmem(at_ends), in_vmem(between), *(in_vmem(x) for x in after))


def half_kernel(which, in_ref, *refs):
    out_ref = refs[-1]
    rows = out_ref.shape[0]
    out_ref[...] = in_ref[which * rows:(which + 1) * rows]


def half_of(x, which, *after):
    vmem = pl.BlockSpec(memory_space=VMEM)
    return pl.pallas_call(
        functools.partial(half_kernel, which),
        out_shape=VMEM((x.shape[0] // 2, x.shape[1]), x.dtype),
        in_specs=[vmem] * (1 + len(after)),
        out_specs=vmem,
        compiler_params=pltpu.CompilerParams(vmem_limit_bytes=8 * 1024 * 1024),
    )(in_vmem(x), *(in_vmem(y) for y in after))


def together(values, *after):
    return lax.optimization_barrier(tuple(values) + after)[: len(values)]


def cycle_of_eight(
    queries, new_keys, new_values, prefix_keys, prefix_values, span_lens, prefix_lens, placement, decode_dest
):
    cycle = lax.axis_size("blk")
    rows = queries.shape[0]
    capacity = 2 * rows // cycle

    def moves(table):
        return [(2 * a + y, 2 * b + y) for a, b in table.items() for y in range(2)]

    swap = [(i, i ^ 1) for i in range(cycle)]
    near = moves({0: 1, 1: 0, 2: 3, 3: 2})
    middle = moves({1: 2, 2: 1})
    ends = moves({0: 3, 3: 0})
    skip = moves({0: 2, 3: 1, 2: 3, 1: 0})
    send = lambda x, table: lax.ppermute(x, "blk", table)

    small = (placement, span_lens, prefix_lens, decode_dest.reshape(cycle, rows))
    own = pack(prefix_keys, prefix_values, new_keys, new_values)
    half = own.shape[0] // 2

    offsets = (0, 2, 1, 6, 3, 4, 7, 5)

    a = send(own, near)
    y_own = send(own, swap)
    b_inner = send(own, middle)
    carry, common = run_first(small, queries, own, offsets, capacity)

    skip_from = choose(own, b_inner)
    a_2, *carry = together((a, *carry))
    y_a = send(a_2, swap)
    own_2, *carry = together((choose(own, own, y_own), *carry))
    b_outer = send(own_2, ends)
    carry = run_stage(common, (1, 2), offsets[1:3], [[a_2], [y_own]], carry, False)

    b = choose(b_outer, choose(b_inner, b_inner, y_a))
    b, *carry = together((b, *carry))
    y_b = send(b, swap)
    skip_from, *carry = together((skip_from, *carry), b, y_a)
    c = send(skip_from, skip)
    carry = run_stage(common, (3, 4), offsets[3:5], [[b], [y_a]], carry, False)

    y_b_high, *carry = together((half_of(y_b, 1), *carry))
    y_c_high = send(y_b_high, near)
    c_low, *carry = together((half_of(c, 0, y_b_high), *carry))
    y_c_low = send(c_low, swap)
    carry = run_stage(common, (5, 6), offsets[5:7], [[c], [y_b]], carry, False)
    return tuple(run_stage(common, (7,), offsets[7:], [[y_c_low, y_c_high]], carry, True))


masked_score = -1e30


def request_of(index, lens):
    ends = jnp.cumsum(lens)
    return jnp.sum((index[:, None] >= ends[None, :]).astype(jnp.int32), axis=1)


def block_rows_for(length):
    chosen = 512
    while length % chosen:
        chosen = chosen // 2
    return chosen


def attend(carried, query_groups, query_req, query_tok, keys, values, key_req, key_tok):
    length = keys.shape[0]
    chosen = block_rows_for(length)
    blocks = length // chosen
    heads_here = query_groups.shape[1]
    score_scale = 1.0 / math.sqrt(HD)
    key_blocks = keys.reshape(blocks, chosen, heads_here, HD)
    value_blocks = values.reshape(blocks, chosen, heads_here, HD)
    req_blocks = key_req.reshape(blocks, chosen)
    tok_blocks = key_tok.reshape(blocks, chosen)

    def one_block(inner, items):
        running_max, running_sum, numerator = inner
        key_part, value_part, req_part, tok_part = items
        visible = (req_part[None, :] == query_req[:, None]) & (
            tok_part[None, :] <= query_tok[:, None]
        )
        scores = (
            jnp.einsum("tkgd,nkd->kgtn", query_groups, key_part, preferred_element_type=jnp.float32)
            * score_scale
        )
        scores = jnp.where(visible, scores, masked_score)
        new_max = jnp.maximum(running_max, jnp.max(scores, axis=-1))
        rescale = jnp.exp(running_max - new_max)
        weights = jnp.where(visible, jnp.exp(scores - new_max[..., None]), 0.0)
        running_sum = running_sum * rescale + jnp.sum(weights, axis=-1)
        numerator = numerator * rescale[..., None] + jnp.einsum(
            "kgtn,nkd->kgtd",
            weights.astype(jnp.bfloat16),
            value_part,
            preferred_element_type=jnp.float32,
        )
        return ((new_max, running_sum, numerator), None)

    result, ignored = lax.scan(
        one_block, carried, (key_blocks, value_blocks, req_blocks, tok_blocks)
    )
    return result


def maybe_attend(
    carried, query_groups, query_req, query_tok, summary, keys, values, key_req, key_tok
):
    query_has, query_last = summary
    request_ids = jnp.arange(query_has.shape[0], dtype=jnp.int32)
    matches = key_req[:, None] == request_ids[None, :]
    wanted = jnp.any(matches & query_has[None, :], axis=1)
    latest = jnp.max(jnp.where(matches, query_last[None, :], -2), axis=1)
    touched = jnp.any(wanted & (key_tok <= latest))
    return lax.cond(
        touched,
        lambda inner: attend(
            inner, query_groups, query_req, query_tok, keys, values, key_req, key_tok
        ),
        lambda inner: inner,
        carried,
    )


def any_cycle(
    queries,
    new_keys,
    new_values,
    prefix_keys,
    prefix_values,
    span_lens,
    prefix_lens,
    placement,
    decode_dest,
):
    cycle_size = lax.axis_size("blk")
    my_index = lax.axis_index("blk")
    rows_here = queries.shape[0]
    kv_cols = new_keys.shape[1]
    heads_here = kv_cols // HD
    groups = H // KVH
    query_groups = queries.reshape(rows_here, heads_here, groups, HD)
    query_tok = lax.dynamic_slice_in_dim(placement, my_index * rows_here, rows_here)
    query_req = request_of(query_tok, span_lens)
    token_req = request_of(placement, span_lens)
    prefix_total = prefix_keys.shape[0] * cycle_size
    prefix_req = request_of(jnp.arange(prefix_total, dtype=jnp.int32), prefix_lens)
    request_ids = jnp.arange(span_lens.shape[0], dtype=jnp.int32)
    member = query_req[:, None] == request_ids[None, :]
    summary = (jnp.any(member, axis=0), jnp.max(jnp.where(member, query_tok[:, None], -1), axis=0))
    initial = (
        jnp.full((heads_here, groups, rows_here), masked_score, jnp.float32),
        jnp.zeros((heads_here, groups, rows_here), jnp.float32),
        jnp.zeros((heads_here, groups, rows_here, HD), jnp.float32),
    )
    piece_keys = lax.all_gather(prefix_keys, "blk", axis=0, tiled=True)
    piece_values = lax.all_gather(prefix_values, "blk", axis=0, tiled=True)
    length = piece_keys.shape[0]
    key_req = prefix_req
    key_tok = jnp.full((length,), -1, jnp.int32)
    carried = maybe_attend(
        initial,
        query_groups,
        query_req,
        query_tok,
        summary,
        piece_keys,
        piece_values,
        key_req,
        key_tok,
    )
    destination = decode_dest[:, 0]
    capacity = 2 * rows_here // cycle_size
    piece_keys = lax.all_gather(new_keys, "blk", axis=0, tiled=True)
    piece_values = lax.all_gather(new_values, "blk", axis=0, tiled=True)
    key_req = token_req
    key_tok = placement
    carried = maybe_attend(
        carried,
        query_groups,
        query_req,
        query_tok,
        summary,
        piece_keys,
        piece_values,
        key_req,
        key_tok,
    )
    local_dest = lax.dynamic_slice_in_dim(destination, my_index * rows_here, rows_here)
    one_hot = (local_dest[:, None] == jnp.arange(cycle_size, dtype=jnp.int32)[None, :]).astype(
        jnp.int32
    )
    slot_rank = jnp.sum(jnp.cumsum(one_hot, axis=0) * one_hot, axis=1) - 1
    target = local_dest * capacity + slot_rank
    selector = (
        jnp.arange(cycle_size * capacity, dtype=jnp.int32)[:, None] == target[None, :]
    ).astype(jnp.bfloat16)
    stacked = jnp.concatenate([new_keys, new_values], axis=1)
    outgoing = jnp.dot(selector, stacked, preferred_element_type=jnp.float32).astype(jnp.bfloat16)
    moved = lax.all_to_all(outgoing, "blk", split_axis=0, concat_axis=0, tiled=True)
    running_max, running_sum, numerator = carried
    attended = (
        (numerator / running_sum[..., None])
        .transpose(2, 0, 1, 3)
        .reshape(rows_here, heads_here * groups * HD)
        .astype(jnp.bfloat16)
    )
    return (attended, moved[:, :kv_cols], moved[:, kv_cols:])


def solution(mesh):
    rows = P(("groups", "blk"), "tensor")
    return jax.shard_map(
        cycle_of_eight if mesh.shape["blk"] == 8 else any_cycle,
        mesh=mesh,
        in_specs=(rows,) * 5 + (P("groups"),) * 3 + (P("groups", None),),
        out_specs=(rows,) * 3,
        check_vma=False,
    )
```

```python
import functools
import math

import jax
import jax.numpy as jnp
from jax import lax
from jax.experimental import pallas as pl
from jax.experimental.pallas import tpu as pltpu
from jax.sharding import PartitionSpec as P

H = 64
KVH = 8
HD = 128
PIECE = 64
LARGE_NEGATIVE = -1e30

VMEM = pltpu.VMEM
SMEM = pltpu.SMEM
HBM = pltpu.HBM


def dot_nt(a, b):
    return lax.dot_general(a, b, (((1,), (1,)), ((), ())), preferred_element_type=jnp.float32)


def dot_nn(a, b):
    return lax.dot_general(a, b, (((1,), (0,)), ((), ())), preferred_element_type=jnp.float32)


def part_of(block, which, rows, start, size):
    if len(block) == 1:
        return block[0][which * rows:(which + 1) * rows, start:start + size]
    half, inner = divmod(which, 2)
    return block[half][inner * rows:(inner + 1) * rows, start:start + size]


def add_blocks(blocks, biases, query_ref, before, after, heads, groups, store):
    rows = query_ref.shape[0]
    factor = math.log2(math.e) / math.sqrt(HD)
    step = 2
    for k in range(heads):
        keys, values = [], []
        for block in blocks:
            keys.append(
                jnp.concatenate(
                    [part_of(block, j, rows, k * HD, HD) for j in (0, 2)], axis=0
                )
            )
            value = jnp.concatenate(
                [part_of(block, j, rows, k * HD, HD) for j in (1, 3)], axis=0
            )
            values.append(jnp.concatenate([value, jnp.ones_like(value)], axis=1))
        for g in range(0, groups, step):
            query = jnp.concatenate(
                [
                    query_ref[:, (k * groups + g + j) * HD:(k * groups + g + j + 1) * HD]
                    for j in range(step)
                ],
                axis=0,
            )
            at = slice(g * rows, (g + step) * rows)
            scores = []
            for key, bias in zip(keys, biases):
                score = (dot_nt(query, key) * factor).reshape(step, rows, 2 * rows) + bias[...][None]
                scores.append(score.reshape(step * rows, 2 * rows))
            largest = functools.reduce(jnp.maximum, scores)
            new_max = jnp.broadcast_to(
                jnp.max(largest, axis=1, keepdims=True), (step * rows, HD)
            )
            if before is not None:
                old_max = before[0][k, at, :]
                new_max = jnp.maximum(old_max, new_max)
            both_max = jnp.concatenate([new_max, new_max], axis=1)
            added = None
            for score, value in zip(scores, values):
                weights = jnp.exp2(score - both_max).astype(jnp.bfloat16)
                term = dot_nn(weights, value)
                added = term if added is None else added + term
            if before is not None:
                rescale = jnp.exp2(old_max - new_max)
                rescale = jnp.concatenate([rescale, rescale], axis=1)
                added = before[1][k, at, :] * rescale + added
            if after is not None:
                after[0][k, at, :] = new_max
                after[1][k, at, :] = added
            else:
                for j in range(step):
                    both = added[j * rows:(j + 1) * rows]
                    store(k, g + j, both[:, :HD] / both[:, HD:])
        if after is None:
            store(k, None, None)


def pick_rows(offsets, blocks, choose_refs, out_refs, picked_ref, sems):
    me = lax.axis_index("blk")
    copies = []
    for n, (offset, block, choose_ref) in enumerate(zip(offsets, blocks, choose_refs)):
        capacity, rows = choose_ref.shape
        index = me ^ offset
        for which, out_ref in enumerate(out_refs):
            new = part_of(block, 2 + which, rows, 0, out_ref.shape[1])
            picked_ref[n, which] = dot_nn(choose_ref[...], new).astype(jnp.bfloat16)
            copy = pltpu.make_async_copy(
                picked_ref.at[n, which],
                out_ref.at[pl.ds(pl.multiple_of(index * capacity, capacity), capacity)],
                sems.at[n, which],
            )
            copy.start()
            copies.append(copy)
    return copies


def first_kernel(
    offsets, rows, heads, groups, requests, capacity,
    place_in, span_in, plen_in, dest_in, query_in, own_ref,
    max_ref, acc_ref, dkey_ref, dval_ref, query_ref, bias_ref, choose_ref,
    place_ref, span_ref, plen_ref, dest_ref, picked_ref, sems, small_sems,
):
    small = [
        pltpu.make_async_copy(source, target, small_sems.at[j])
        for j, (source, target) in enumerate(
            (
                (place_in, place_ref),
                (span_in, span_ref),
                (plen_in, plen_ref),
                (dest_in, dest_ref),
                (query_in, query_ref),
            )
        )
    ]
    for copy in small:
        copy.start()
    for copy in small:
        copy.wait()
    me = lax.axis_index("blk")
    pieces = rows // PIECE

    def bounds(token):
        low = jnp.zeros_like(token)
        pre_low = jnp.zeros_like(token)
        pre_high = jnp.zeros_like(token) + plen_ref[0]
        end = jnp.int32(0)
        for r in range(requests - 1):
            end = end + span_ref[r]
            past = token >= end
            low = low + jnp.where(past, span_ref[r], 0)
            pre_low = pre_low + jnp.where(past, plen_ref[r], 0)
            pre_high = pre_high + jnp.where(past, plen_ref[r + 1], 0)
        return low, pre_low, pre_high

    def tokens_of(index, shape, axis):
        place = lax.broadcasted_iota(jnp.int32, shape, axis)
        token = place
        for piece in range(pieces):
            start = place_ref[index * rows + piece * PIECE] - piece * PIECE
            token = jnp.where(place >= piece * PIECE, place + start, token)
        return token

    token = tokens_of(me, (rows, rows), 0)
    low, pre_low, pre_high = bounds(token)
    column = lax.broadcasted_iota(jnp.int32, (rows, rows), 1)
    earlier = jnp.where(lax.broadcasted_iota(jnp.int32, (rows, rows), 0) < column, 1.0, 0.0)
    earlier = earlier.astype(jnp.bfloat16)
    slot = lax.broadcasted_iota(jnp.int32, (capacity, rows), 0).astype(jnp.float32)
    for n, offset in enumerate(offsets):
        index = me ^ offset
        position = column + index * rows
        pre_seen = (position >= pre_low) & (position < pre_high)
        key_token = tokens_of(index, (rows, rows), 1)
        new_seen = (key_token >= low) & (key_token <= token)
        bias_ref[n, :, :rows] = jnp.where(pre_seen, 0.0, LARGE_NEGATIVE).astype(jnp.float32)
        bias_ref[n, :, rows:] = jnp.where(new_seen, 0.0, LARGE_NEGATIVE).astype(jnp.float32)
        mine = jnp.where(dest_ref[pl.ds(index, 1), :] == me, 1.0, 0.0)
        mine = jnp.broadcast_to(mine, (capacity, rows))
        rank = dot_nn(mine.astype(jnp.bfloat16), earlier)
        choose_ref[n] = jnp.where((rank == slot) & (mine > 0.5), 1.0, 0.0).astype(jnp.bfloat16)
    copies = pick_rows(
        (0,), [[own_ref]], [choose_ref.at[0]], (dkey_ref, dval_ref), picked_ref, sems
    )
    add_blocks(
        [[own_ref]], [bias_ref.at[0]], query_ref, None, (max_ref, acc_ref), heads, groups, None
    )
    for copy in copies:
        copy.wait()


def stage_kernel(order, offsets, parts, last, heads, groups, *refs):
    refs = list(refs)
    query_ref, bias_ref, choose_ref = refs[:3]
    refs = refs[3:]
    blocks = []
    for count in parts:
        blocks.append(refs[:count])
        refs = refs[count:]
    before = refs[:2]
    refs = refs[4:]
    if last:
        att_ref, dkey_ref, dval_ref, picked_ref, sems, att_vmem, att_sems = refs
        after = None
    else:
        max_ref, acc_ref, dkey_ref, dval_ref, picked_ref, sems = refs
        after = (max_ref, acc_ref)
    copies = pick_rows(
        offsets, blocks, [choose_ref.at[n] for n in order], (dkey_ref, dval_ref), picked_ref, sems
    )

    def store(k, g, result):
        if g is not None:
            att_vmem[:, (k * groups + g) * HD:(k * groups + g + 1) * HD] = result.astype(jnp.bfloat16)
            return
        columns = slice(k * groups * HD, (k + 1) * groups * HD)
        copy = pltpu.make_async_copy(
            att_vmem.at[:, columns], att_ref.at[:, columns], att_sems.at[k]
        )
        copy.start()
        copies.append(copy)

    add_blocks(
        blocks, [bias_ref.at[n] for n in order], query_ref, before, after, heads, groups, store
    )
    for copy in copies:
        copy.wait()


def in_vmem(x):
    return pltpu.with_memory_space_constraint(x, VMEM)


def shapes_of(rows, columns, cycle):
    groups = H // KVH
    heads = columns // (groups * HD)
    state = (
        VMEM((heads, groups * rows, HD), jnp.float32),
        VMEM((heads, groups * rows, 2 * HD), jnp.float32),
    )
    decode = jax.ShapeDtypeStruct((2 * rows, heads * HD), jnp.bfloat16)
    return groups, heads, state, (decode, decode)


def params(keys, rows, columns):
    return dict(
        compiler_params=pltpu.CompilerParams(vmem_limit_bytes=20 * 1024 * 1024),
        cost_estimate=pl.CostEstimate(
            flops=4 * rows * columns * keys, bytes_accessed=4 * 1024 * 1024, transcendentals=0
        ),
    )


def run_first(small, query, own, offsets, capacity):
    rows, columns = query.shape
    cycle = len(offsets)
    groups, heads, state, decode = shapes_of(rows, columns, cycle)
    hbm, vmem = pl.BlockSpec(memory_space=HBM), pl.BlockSpec(memory_space=VMEM)
    small = tuple(pltpu.with_memory_space_constraint(x, HBM) for x in small)
    *state, dkey, dval, query, bias, choose = pl.pallas_call(
        functools.partial(
            first_kernel, offsets, rows, heads, groups, small[1].shape[0], capacity
        ),
        out_shape=(
            *state,
            *decode,
            VMEM((rows, columns), jnp.bfloat16),
            VMEM((cycle, rows, 2 * rows), jnp.float32),
            VMEM((cycle, capacity, rows), jnp.bfloat16),
        ),
        in_specs=[hbm] * 5 + [vmem],
        out_specs=(vmem, vmem, hbm, hbm, vmem, vmem, vmem),
        scratch_shapes=[
            *[SMEM(x.shape, jnp.int32) for x in small[:3]],
            VMEM(small[3].shape, jnp.int32),
            VMEM((1, 2, capacity, heads * HD), jnp.bfloat16),
            pltpu.SemaphoreType.DMA((1, 2)),
            pltpu.SemaphoreType.DMA((5,)),
        ],
        **params(2 * rows, rows, columns),
    )(*small, pltpu.with_memory_space_constraint(query, HBM), in_vmem(own))
    return [*state, dkey, dval], (query, bias, choose)


def run_stage(common, order, offsets, blocks, carry, last):
    rows, columns = common[0].shape
    cycle, capacity, unused = common[2].shape
    groups, heads, state, decode = shapes_of(rows, columns, cycle)
    parts = tuple(len(block) for block in blocks)
    flat = [in_vmem(ref) for block in blocks for ref in block]
    hbm, vmem = pl.BlockSpec(memory_space=HBM), pl.BlockSpec(memory_space=VMEM)
    operands = [*(in_vmem(x) for x in common), *flat]
    at = len(operands)
    operands += [in_vmem(carry[0]), in_vmem(carry[1]), *carry[2:]]
    scratch = [
        VMEM((len(blocks), 2, capacity, heads * HD), jnp.bfloat16),
        pltpu.SemaphoreType.DMA((len(blocks), 2)),
    ]
    if last:
        out_shape = (jax.ShapeDtypeStruct((rows, columns), jnp.bfloat16), *decode)
        out_specs = (hbm, hbm, hbm)
        alias = {at + 2: 1, at + 3: 2}
        scratch += [VMEM((rows, columns), jnp.bfloat16), pltpu.SemaphoreType.DMA((heads,))]
    else:
        out_shape = (*state, *decode)
        out_specs = (vmem, vmem, hbm, hbm)
        alias = {at + j: j for j in range(4)}
    return pl.pallas_call(
        functools.partial(stage_kernel, order, offsets, parts, last, heads, groups),
        out_shape=out_shape,
        in_specs=[vmem] * (at + 2) + [hbm] * 2,
        out_specs=out_specs,
        input_output_aliases=alias,
        scratch_shapes=scratch,
        **params(2 * rows * len(blocks), rows, columns),
    )(*operands)


def pack_kernel(*refs):
    *inputs, out_ref, sems = refs
    rows = inputs[0].shape[0]
    copies = [
        pltpu.make_async_copy(ref, out_ref.at[j * rows:(j + 1) * rows], sems.at[j])
        for j, ref in enumerate(inputs)
    ]
    for copy in copies:
        copy.start()
    for copy in copies:
        copy.wait()


def pack(*arrays):
    rows, columns = arrays[0].shape
    return pl.pallas_call(
        pack_kernel,
        out_shape=VMEM((rows * len(arrays), columns), jnp.bfloat16),
        in_specs=[pl.BlockSpec(memory_space=HBM)] * len(arrays),
        out_specs=pl.BlockSpec(memory_space=VMEM),
        scratch_shapes=[pltpu.SemaphoreType.DMA((len(arrays),))],
        compiler_params=pltpu.CompilerParams(vmem_limit_bytes=4 * 1024 * 1024),
    )(*(pltpu.with_memory_space_constraint(x, HBM) for x in arrays))


def choose_kernel(at_ends, between, *refs):
    out_ref = refs[-1]
    place = lax.axis_index("blk") // 2
    outer = (place == 0) | (place == 3)

    @pl.when(outer)
    def _():
        out_ref[...] = at_ends[...]

    @pl.when(jnp.logical_not(outer))
    def _():
        out_ref[...] = between[...]


def choose(at_ends, between, *after):
    vmem = pl.BlockSpec(memory_space=VMEM)
    return pl.pallas_call(
        choose_kernel,
        out_shape=VMEM(at_ends.shape, at_ends.dtype),
        in_specs=[vmem] * (2 + len(after)),
        out_specs=vmem,
        compiler_params=pltpu.CompilerParams(vmem_limit_bytes=8 * 1024 * 1024),
    )(in_vmem(at_ends), in_vmem(between), *(in_vmem(x) for x in after))


def half_kernel(which, in_ref, *refs):
    out_ref = refs[-1]
    rows = out_ref.shape[0]
    out_ref[...] = in_ref[which * rows:(which + 1) * rows]


def half_of(x, which, *after):
    vmem = pl.BlockSpec(memory_space=VMEM)
    return pl.pallas_call(
        functools.partial(half_kernel, which),
        out_shape=VMEM((x.shape[0] // 2, x.shape[1]), x.dtype),
        in_specs=[vmem] * (1 + len(after)),
        out_specs=vmem,
        compiler_params=pltpu.CompilerParams(vmem_limit_bytes=8 * 1024 * 1024),
    )(in_vmem(x), *(in_vmem(y) for y in after))


def together(values, *after):
    return lax.optimization_barrier(tuple(values) + after)[: len(values)]


def cycle_of_eight(
    queries, new_keys, new_values, prefix_keys, prefix_values, span_lens, prefix_lens, placement, decode_dest
):
    cycle = lax.axis_size("blk")
    rows = queries.shape[0]
    capacity = 2 * rows // cycle

    def moves(table):
        return [(2 * a + y, 2 * b + y) for a, b in table.items() for y in range(2)]

    swap = [(i, i ^ 1) for i in range(cycle)]
    near = moves({0: 1, 1: 0, 2: 3, 3: 2})
    middle = moves({1: 2, 2: 1})
    ends = moves({0: 3, 3: 0})
    skip = moves({0: 2, 3: 1, 2: 3, 1: 0})
    send = lambda x, table: lax.ppermute(x, "blk", table)

    small = (placement, span_lens, prefix_lens, decode_dest.reshape(cycle, rows))
    own = pack(prefix_keys, prefix_values, new_keys, new_values)
    half = own.shape[0] // 2

    offsets = (0, 2, 1, 6, 3, 4, 7, 5)

    a = send(own, near)
    y_own = send(own, swap)
    b_inner = send(own, middle)
    carry, common = run_first(small, queries, own, offsets, capacity)

    own_2, *carry = together((choose(own, own, a), *carry))
    b_outer = send(own_2, ends)
    a_2, *carry = together((choose(a, a, y_own, own_2), *carry))
    y_a = send(a_2, swap)
    carry = run_stage(common, (1, 2), offsets[1:3], [[a], [y_own]], carry, False)

    skip_from = choose(own, b_inner)
    b = choose(b_outer, b_inner)
    b, *carry = together((choose(b, b, y_a), *carry))
    y_b = send(b, swap)
    skip_from, *carry = together((skip_from, *carry), b, y_a)
    c = send(skip_from, skip)
    carry = run_stage(common, (3, 4), offsets[3:5], [[b], [y_a]], carry, False)

    y_b_high, *carry = together((half_of(y_b, 1), *carry))
    y_c_high = send(y_b_high, near)
    c_low, *carry = together((half_of(c, 0, y_b_high), *carry))
    y_c_low = send(c_low, swap)
    carry = run_stage(common, (5, 6), offsets[5:7], [[c], [y_b]], carry, False)
    return tuple(run_stage(common, (7,), offsets[7:], [[y_c_low, y_c_high]], carry, True))


masked_score = -1e30


def request_of(index, lens):
    ends = jnp.cumsum(lens)
    return jnp.sum((index[:, None] >= ends[None, :]).astype(jnp.int32), axis=1)


def block_rows_for(length):
    chosen = 512
    while length % chosen:
        chosen = chosen // 2
    return chosen


def attend(carried, query_groups, query_req, query_tok, keys, values, key_req, key_tok):
    length = keys.shape[0]
    chosen = block_rows_for(length)
    blocks = length // chosen
    heads_here = query_groups.shape[1]
    score_scale = 1.0 / math.sqrt(HD)
    key_blocks = keys.reshape(blocks, chosen, heads_here, HD)
    value_blocks = values.reshape(blocks, chosen, heads_here, HD)
    req_blocks = key_req.reshape(blocks, chosen)
    tok_blocks = key_tok.reshape(blocks, chosen)

    def one_block(inner, items):
        running_max, running_sum, numerator = inner
        key_part, value_part, req_part, tok_part = items
        visible = (req_part[None, :] == query_req[:, None]) & (
            tok_part[None, :] <= query_tok[:, None]
        )
        scores = (
            jnp.einsum("tkgd,nkd->kgtn", query_groups, key_part, preferred_element_type=jnp.float32)
            * score_scale
        )
        scores = jnp.where(visible, scores, masked_score)
        new_max = jnp.maximum(running_max, jnp.max(scores, axis=-1))
        rescale = jnp.exp(running_max - new_max)
        weights = jnp.where(visible, jnp.exp(scores - new_max[..., None]), 0.0)
        running_sum = running_sum * rescale + jnp.sum(weights, axis=-1)
        numerator = numerator * rescale[..., None] + jnp.einsum(
            "kgtn,nkd->kgtd",
            weights.astype(jnp.bfloat16),
            value_part,
            preferred_element_type=jnp.float32,
        )
        return ((new_max, running_sum, numerator), None)

    result, ignored = lax.scan(
        one_block, carried, (key_blocks, value_blocks, req_blocks, tok_blocks)
    )
    return result


def maybe_attend(
    carried, query_groups, query_req, query_tok, summary, keys, values, key_req, key_tok
):
    query_has, query_last = summary
    request_ids = jnp.arange(query_has.shape[0], dtype=jnp.int32)
    matches = key_req[:, None] == request_ids[None, :]
    wanted = jnp.any(matches & query_has[None, :], axis=1)
    latest = jnp.max(jnp.where(matches, query_last[None, :], -2), axis=1)
    touched = jnp.any(wanted & (key_tok <= latest))
    return lax.cond(
        touched,
        lambda inner: attend(
            inner, query_groups, query_req, query_tok, keys, values, key_req, key_tok
        ),
        lambda inner: inner,
        carried,
    )


def any_cycle(
    queries,
    new_keys,
    new_values,
    prefix_keys,
    prefix_values,
    span_lens,
    prefix_lens,
    placement,
    decode_dest,
):
    cycle_size = lax.axis_size("blk")
    my_index = lax.axis_index("blk")
    rows_here = queries.shape[0]
    kv_cols = new_keys.shape[1]
    heads_here = kv_cols // HD
    groups = H // KVH
    query_groups = queries.reshape(rows_here, heads_here, groups, HD)
    query_tok = lax.dynamic_slice_in_dim(placement, my_index * rows_here, rows_here)
    query_req = request_of(query_tok, span_lens)
    token_req = request_of(placement, span_lens)
    prefix_total = prefix_keys.shape[0] * cycle_size
    prefix_req = request_of(jnp.arange(prefix_total, dtype=jnp.int32), prefix_lens)
    request_ids = jnp.arange(span_lens.shape[0], dtype=jnp.int32)
    member = query_req[:, None] == request_ids[None, :]
    summary = (jnp.any(member, axis=0), jnp.max(jnp.where(member, query_tok[:, None], -1), axis=0))
    initial = (
        jnp.full((heads_here, groups, rows_here), masked_score, jnp.float32),
        jnp.zeros((heads_here, groups, rows_here), jnp.float32),
        jnp.zeros((heads_here, groups, rows_here, HD), jnp.float32),
    )
    piece_keys = lax.all_gather(prefix_keys, "blk", axis=0, tiled=True)
    piece_values = lax.all_gather(prefix_values, "blk", axis=0, tiled=True)
    length = piece_keys.shape[0]
    key_req = prefix_req
    key_tok = jnp.full((length,), -1, jnp.int32)
    carried = maybe_attend(
        initial,
        query_groups,
        query_req,
        query_tok,
        summary,
        piece_keys,
        piece_values,
        key_req,
        key_tok,
    )
    destination = decode_dest[:, 0]
    capacity = 2 * rows_here // cycle_size
    piece_keys = lax.all_gather(new_keys, "blk", axis=0, tiled=True)
    piece_values = lax.all_gather(new_values, "blk", axis=0, tiled=True)
    key_req = token_req
    key_tok = placement
    carried = maybe_attend(
        carried,
        query_groups,
        query_req,
        query_tok,
        summary,
        piece_keys,
        piece_values,
        key_req,
        key_tok,
    )
    local_dest = lax.dynamic_slice_in_dim(destination, my_index * rows_here, rows_here)
    one_hot = (local_dest[:, None] == jnp.arange(cycle_size, dtype=jnp.int32)[None, :]).astype(
        jnp.int32
    )
    slot_rank = jnp.sum(jnp.cumsum(one_hot, axis=0) * one_hot, axis=1) - 1
    target = local_dest * capacity + slot_rank
    selector = (
        jnp.arange(cycle_size * capacity, dtype=jnp.int32)[:, None] == target[None, :]
    ).astype(jnp.bfloat16)
    stacked = jnp.concatenate([new_keys, new_values], axis=1)
    outgoing = jnp.dot(selector, stacked, preferred_element_type=jnp.float32).astype(jnp.bfloat16)
    moved = lax.all_to_all(outgoing, "blk", split_axis=0, concat_axis=0, tiled=True)
    running_max, running_sum, numerator = carried
    attended = (
        (numerator / running_sum[..., None])
        .transpose(2, 0, 1, 3)
        .reshape(rows_here, heads_here * groups * HD)
        .astype(jnp.bfloat16)
    )
    return (attended, moved[:, :kv_cols], moved[:, kv_cols:])


def solution(mesh):
    rows = P(("groups", "blk"), "tensor")
    return jax.shard_map(
        cycle_of_eight if mesh.shape["blk"] == 8 else any_cycle,
        mesh=mesh,
        in_specs=(rows,) * 5 + (P("groups"),) * 3 + (P("groups", None),),
        out_specs=(rows,) * 3,
        check_vma=False,
    )
```

```python
import functools
import math

import jax
import jax.numpy as jnp
from jax import lax
from jax.experimental import pallas as pl
from jax.experimental.pallas import tpu as pltpu
from jax.sharding import PartitionSpec as P

H = 64
KVH = 8
HD = 128
PIECE = 64
LARGE_NEGATIVE = -1e30

VMEM = pltpu.VMEM
SMEM = pltpu.SMEM
HBM = pltpu.HBM


def dot_nt(a, b):
    return lax.dot_general(a, b, (((1,), (1,)), ((), ())), preferred_element_type=jnp.float32)


def dot_nn(a, b):
    return lax.dot_general(a, b, (((1,), (0,)), ((), ())), preferred_element_type=jnp.float32)


def part_of(block, which, rows, start, size):
    if len(block) == 1:
        return block[0][which * rows:(which + 1) * rows, start:start + size]
    half, inner = divmod(which, 2)
    return block[half][inner * rows:(inner + 1) * rows, start:start + size]


def add_blocks(blocks, biases, query_ref, before, after, heads, groups, store):
    rows = query_ref.shape[0]
    factor = math.log2(math.e) / math.sqrt(HD)
    step = 2
    for k in range(heads):
        keys, values = [], []
        for block in blocks:
            keys.append(
                jnp.concatenate(
                    [part_of(block, j, rows, k * HD, HD) for j in (0, 2)], axis=0
                )
            )
            value = jnp.concatenate(
                [part_of(block, j, rows, k * HD, HD) for j in (1, 3)], axis=0
            )
            values.append(jnp.concatenate([value, jnp.ones_like(value)], axis=1))
        for g in range(0, groups, step):
            query = jnp.concatenate(
                [
                    query_ref[:, (k * groups + g + j) * HD:(k * groups + g + j + 1) * HD]
                    for j in range(step)
                ],
                axis=0,
            )
            at = slice(g * rows, (g + step) * rows)
            scores = []
            for key, bias in zip(keys, biases):
                score = (dot_nt(query, key) * factor).reshape(step, rows, 2 * rows) + bias[...][None]
                scores.append(score.reshape(step * rows, 2 * rows))
            largest = functools.reduce(jnp.maximum, scores)
            new_max = jnp.broadcast_to(
                jnp.max(largest, axis=1, keepdims=True), (step * rows, HD)
            )
            if before is not None:
                old_max = before[0][k, at, :]
                new_max = jnp.maximum(old_max, new_max)
            both_max = jnp.concatenate([new_max, new_max], axis=1)
            added = None
            for score, value in zip(scores, values):
                weights = jnp.exp2(score - both_max).astype(jnp.bfloat16)
                term = dot_nn(weights, value)
                added = term if added is None else added + term
            if before is not None:
                rescale = jnp.exp2(old_max - new_max)
                rescale = jnp.concatenate([rescale, rescale], axis=1)
                added = before[1][k, at, :] * rescale + added
            if after is not None:
                after[0][k, at, :] = new_max
                after[1][k, at, :] = added
            else:
                for j in range(step):
                    both = added[j * rows:(j + 1) * rows]
                    store(k, g + j, both[:, :HD] / both[:, HD:])
        if after is None:
            store(k, None, None)


def pick_rows(offsets, blocks, choose_refs, out_refs, picked_ref, sems):
    me = lax.axis_index("blk")
    copies = []
    for n, (offset, block, choose_ref) in enumerate(zip(offsets, blocks, choose_refs)):
        capacity, rows = choose_ref.shape
        index = me ^ offset
        for which, out_ref in enumerate(out_refs):
            new = part_of(block, 2 + which, rows, 0, out_ref.shape[1])
            picked_ref[n, which] = dot_nn(choose_ref[...], new).astype(jnp.bfloat16)
            copy = pltpu.make_async_copy(
                picked_ref.at[n, which],
                out_ref.at[pl.ds(pl.multiple_of(index * capacity, capacity), capacity)],
                sems.at[n, which],
            )
            copy.start()
            copies.append(copy)
    return copies


def first_kernel(
    offsets, rows, heads, groups, requests, capacity,
    place_in, span_in, plen_in, dest_in, query_in, own_ref,
    max_ref, acc_ref, dkey_ref, dval_ref, query_ref, bias_ref, choose_ref,
    place_ref, span_ref, plen_ref, dest_ref, picked_ref, sems, small_sems,
):
    small = [
        pltpu.make_async_copy(source, target, small_sems.at[j])
        for j, (source, target) in enumerate(
            (
                (place_in, place_ref),
                (span_in, span_ref),
                (plen_in, plen_ref),
                (dest_in, dest_ref),
                (query_in, query_ref),
            )
        )
    ]
    for copy in small:
        copy.start()
    for copy in small:
        copy.wait()
    me = lax.axis_index("blk")
    pieces = rows // PIECE

    def bounds(token):
        low = jnp.zeros_like(token)
        pre_low = jnp.zeros_like(token)
        pre_high = jnp.zeros_like(token) + plen_ref[0]
        end = jnp.int32(0)
        for r in range(requests - 1):
            end = end + span_ref[r]
            past = token >= end
            low = low + jnp.where(past, span_ref[r], 0)
            pre_low = pre_low + jnp.where(past, plen_ref[r], 0)
            pre_high = pre_high + jnp.where(past, plen_ref[r + 1], 0)
        return low, pre_low, pre_high

    def tokens_of(index, shape, axis):
        place = lax.broadcasted_iota(jnp.int32, shape, axis)
        token = place
        for piece in range(pieces):
            start = place_ref[index * rows + piece * PIECE] - piece * PIECE
            token = jnp.where(place >= piece * PIECE, place + start, token)
        return token

    token = tokens_of(me, (rows, rows), 0)
    low, pre_low, pre_high = bounds(token)
    column = lax.broadcasted_iota(jnp.int32, (rows, rows), 1)
    earlier = jnp.where(lax.broadcasted_iota(jnp.int32, (rows, rows), 0) < column, 1.0, 0.0)
    earlier = earlier.astype(jnp.bfloat16)
    slot = lax.broadcasted_iota(jnp.int32, (capacity, rows), 0).astype(jnp.float32)
    for n, offset in enumerate(offsets):
        index = me ^ offset
        position = column + index * rows
        pre_seen = (position >= pre_low) & (position < pre_high)
        key_token = tokens_of(index, (rows, rows), 1)
        new_seen = (key_token >= low) & (key_token <= token)
        bias_ref[n, :, :rows] = jnp.where(pre_seen, 0.0, LARGE_NEGATIVE).astype(jnp.float32)
        bias_ref[n, :, rows:] = jnp.where(new_seen, 0.0, LARGE_NEGATIVE).astype(jnp.float32)
        mine = jnp.where(dest_ref[pl.ds(index, 1), :] == me, 1.0, 0.0)
        mine = jnp.broadcast_to(mine, (capacity, rows))
        rank = dot_nn(mine.astype(jnp.bfloat16), earlier)
        choose_ref[n] = jnp.where((rank == slot) & (mine > 0.5), 1.0, 0.0).astype(jnp.bfloat16)
    copies = pick_rows(
        (0,), [[own_ref]], [choose_ref.at[0]], (dkey_ref, dval_ref), picked_ref, sems
    )
    add_blocks(
        [[own_ref]], [bias_ref.at[0]], query_ref, None, (max_ref, acc_ref), heads, groups, None
    )
    for copy in copies:
        copy.wait()


def stage_kernel(order, offsets, parts, last, heads, groups, *refs):
    refs = list(refs)
    query_ref, bias_ref, choose_ref = refs[:3]
    refs = refs[3:]
    blocks = []
    for count in parts:
        blocks.append(refs[:count])
        refs = refs[count:]
    before = refs[:2]
    refs = refs[4:]
    if last:
        att_ref, dkey_ref, dval_ref, picked_ref, sems, att_vmem, att_sems = refs
        after = None
    else:
        max_ref, acc_ref, dkey_ref, dval_ref, picked_ref, sems = refs
        after = (max_ref, acc_ref)
    copies = pick_rows(
        offsets, blocks, [choose_ref.at[n] for n in order], (dkey_ref, dval_ref), picked_ref, sems
    )

    def store(k, g, result):
        if g is not None:
            att_vmem[:, (k * groups + g) * HD:(k * groups + g + 1) * HD] = result.astype(jnp.bfloat16)
            return
        columns = slice(k * groups * HD, (k + 1) * groups * HD)
        copy = pltpu.make_async_copy(
            att_vmem.at[:, columns], att_ref.at[:, columns], att_sems.at[k]
        )
        copy.start()
        copies.append(copy)

    add_blocks(
        blocks, [bias_ref.at[n] for n in order], query_ref, before, after, heads, groups, store
    )
    for copy in copies:
        copy.wait()


def in_vmem(x):
    return pltpu.with_memory_space_constraint(x, VMEM)


def shapes_of(rows, columns, cycle):
    groups = H // KVH
    heads = columns // (groups * HD)
    state = (
        VMEM((heads, groups * rows, HD), jnp.float32),
        VMEM((heads, groups * rows, 2 * HD), jnp.float32),
    )
    decode = jax.ShapeDtypeStruct((2 * rows, heads * HD), jnp.bfloat16)
    return groups, heads, state, (decode, decode)


def params(keys, rows, columns):
    return dict(
        compiler_params=pltpu.CompilerParams(vmem_limit_bytes=20 * 1024 * 1024),
        cost_estimate=pl.CostEstimate(
            flops=4 * rows * columns * keys, bytes_accessed=4 * 1024 * 1024, transcendentals=0
        ),
    )


def run_first(small, query, own, offsets, capacity):
    rows, columns = query.shape
    cycle = len(offsets)
    groups, heads, state, decode = shapes_of(rows, columns, cycle)
    hbm, vmem = pl.BlockSpec(memory_space=HBM), pl.BlockSpec(memory_space=VMEM)
    small = tuple(pltpu.with_memory_space_constraint(x, HBM) for x in small)
    *state, dkey, dval, query, bias, choose = pl.pallas_call(
        functools.partial(
            first_kernel, offsets, rows, heads, groups, small[1].shape[0], capacity
        ),
        out_shape=(
            *state,
            *decode,
            VMEM((rows, columns), jnp.bfloat16),
            VMEM((cycle, rows, 2 * rows), jnp.float32),
            VMEM((cycle, capacity, rows), jnp.bfloat16),
        ),
        in_specs=[hbm] * 5 + [vmem],
        out_specs=(vmem, vmem, hbm, hbm, vmem, vmem, vmem),
        scratch_shapes=[
            *[SMEM(x.shape, jnp.int32) for x in small[:3]],
            VMEM(small[3].shape, jnp.int32),
            VMEM((1, 2, capacity, heads * HD), jnp.bfloat16),
            pltpu.SemaphoreType.DMA((1, 2)),
            pltpu.SemaphoreType.DMA((5,)),
        ],
        **params(2 * rows, rows, columns),
    )(*small, pltpu.with_memory_space_constraint(query, HBM), in_vmem(own))
    return [*state, dkey, dval], (query, bias, choose)


def run_stage(common, order, offsets, blocks, carry, last):
    rows, columns = common[0].shape
    cycle, capacity, unused = common[2].shape
    groups, heads, state, decode = shapes_of(rows, columns, cycle)
    parts = tuple(len(block) for block in blocks)
    flat = [in_vmem(ref) for block in blocks for ref in block]
    hbm, vmem = pl.BlockSpec(memory_space=HBM), pl.BlockSpec(memory_space=VMEM)
    operands = [*(in_vmem(x) for x in common), *flat]
    at = len(operands)
    operands += [in_vmem(carry[0]), in_vmem(carry[1]), *carry[2:]]
    scratch = [
        VMEM((len(blocks), 2, capacity, heads * HD), jnp.bfloat16),
        pltpu.SemaphoreType.DMA((len(blocks), 2)),
    ]
    if last:
        out_shape = (jax.ShapeDtypeStruct((rows, columns), jnp.bfloat16), *decode)
        out_specs = (hbm, hbm, hbm)
        alias = {at + 2: 1, at + 3: 2}
        scratch += [VMEM((rows, columns), jnp.bfloat16), pltpu.SemaphoreType.DMA((heads,))]
    else:
        out_shape = (*state, *decode)
        out_specs = (vmem, vmem, hbm, hbm)
        alias = {at + j: j for j in range(4)}
    return pl.pallas_call(
        functools.partial(stage_kernel, order, offsets, parts, last, heads, groups),
        out_shape=out_shape,
        in_specs=[vmem] * (at + 2) + [hbm] * 2,
        out_specs=out_specs,
        input_output_aliases=alias,
        scratch_shapes=scratch,
        **params(2 * rows * len(blocks), rows, columns),
    )(*operands)


def pack_kernel(*refs):
    *inputs, out_ref, sems = refs
    rows = inputs[0].shape[0]
    copies = [
        pltpu.make_async_copy(ref, out_ref.at[j * rows:(j + 1) * rows], sems.at[j])
        for j, ref in enumerate(inputs)
    ]
    for copy in copies:
        copy.start()
    for copy in copies:
        copy.wait()


def pack(*arrays):
    rows, columns = arrays[0].shape
    return pl.pallas_call(
        pack_kernel,
        out_shape=VMEM((rows * len(arrays), columns), jnp.bfloat16),
        in_specs=[pl.BlockSpec(memory_space=HBM)] * len(arrays),
        out_specs=pl.BlockSpec(memory_space=VMEM),
        scratch_shapes=[pltpu.SemaphoreType.DMA((len(arrays),))],
        compiler_params=pltpu.CompilerParams(vmem_limit_bytes=4 * 1024 * 1024),
    )(*(pltpu.with_memory_space_constraint(x, HBM) for x in arrays))


def choose_kernel(at_ends, between, *refs):
    out_ref = refs[-1]
    place = lax.axis_index("blk") // 2
    outer = (place == 0) | (place == 3)

    @pl.when(outer)
    def _():
        out_ref[...] = at_ends[...]

    @pl.when(jnp.logical_not(outer))
    def _():
        out_ref[...] = between[...]


def choose(at_ends, between, *after):
    vmem = pl.BlockSpec(memory_space=VMEM)
    return pl.pallas_call(
        choose_kernel,
        out_shape=VMEM(at_ends.shape, at_ends.dtype),
        in_specs=[vmem] * (2 + len(after)),
        out_specs=vmem,
        compiler_params=pltpu.CompilerParams(vmem_limit_bytes=8 * 1024 * 1024),
    )(in_vmem(at_ends), in_vmem(between), *(in_vmem(x) for x in after))


def half_kernel(which, in_ref, *refs):
    out_ref = refs[-1]
    rows = out_ref.shape[0]
    out_ref[...] = in_ref[which * rows:(which + 1) * rows]


def half_of(x, which, *after):
    vmem = pl.BlockSpec(memory_space=VMEM)
    return pl.pallas_call(
        functools.partial(half_kernel, which),
        out_shape=VMEM((x.shape[0] // 2, x.shape[1]), x.dtype),
        in_specs=[vmem] * (1 + len(after)),
        out_specs=vmem,
        compiler_params=pltpu.CompilerParams(vmem_limit_bytes=8 * 1024 * 1024),
    )(in_vmem(x), *(in_vmem(y) for y in after))


def together(values, *after):
    return lax.optimization_barrier(tuple(values) + after)[: len(values)]


def cycle_of_eight(
    queries, new_keys, new_values, prefix_keys, prefix_values, span_lens, prefix_lens, placement, decode_dest
):
    cycle = lax.axis_size("blk")
    rows = queries.shape[0]
    capacity = 2 * rows // cycle

    def moves(table):
        return [(2 * a + y, 2 * b + y) for a, b in table.items() for y in range(2)]

    swap = [(i, i ^ 1) for i in range(cycle)]
    near = moves({0: 1, 1: 0, 2: 3, 3: 2})
    middle = moves({1: 2, 2: 1})
    ends = moves({0: 3, 3: 0})
    skip = moves({0: 2, 3: 1, 2: 3, 1: 0})
    send = lambda x, table: lax.ppermute(x, "blk", table)

    small = (placement, span_lens, prefix_lens, decode_dest.reshape(cycle, rows))
    own = pack(prefix_keys, prefix_values, new_keys, new_values)
    half = own.shape[0] // 2

    offsets = (0, 2, 1, 6, 3, 4, 7, 5)

    a = send(own, near)
    y_own = send(own, swap)
    b_inner = send(own, middle)
    carry, common = run_first(small, queries, own, offsets, capacity)

    own_2, *carry = together((choose(own, own, a), *carry))
    b_outer = send(own_2, ends)
    a_2, *carry = together((choose(a, a, y_own, own_2), *carry))
    y_a = send(a_2, swap)
    carry = run_stage(common, (1, 2), offsets[1:3], [[a], [y_own]], carry, False)

    skip_from, *carry = together((choose(own, b_inner, b_outer), *carry))
    c = send(skip_from, skip)
    b_outer, *carry = together((b_outer, *carry), skip_from)
    b = choose(b_outer, b_inner, y_a)
    y_b = send(b, swap)
    carry = run_stage(common, (3, 4), offsets[3:5], [[b], [y_a]], carry, False)

    c_low = half_of(c, 0, carry[0])
    y_c_low = send(c_low, swap)
    y_b_high, *carry = together((half_of(y_b, 1, c_low), *carry))
    y_c_high = send(y_b_high, near)
    carry = run_stage(common, (5, 6), offsets[5:7], [[c], [y_b]], carry, False)
    return tuple(run_stage(common, (7,), offsets[7:], [[y_c_low, y_c_high]], carry, True))


masked_score = -1e30


def request_of(index, lens):
    ends = jnp.cumsum(lens)
    return jnp.sum((index[:, None] >= ends[None, :]).astype(jnp.int32), axis=1)


def block_rows_for(length):
    chosen = 512
    while length % chosen:
        chosen = chosen // 2
    return chosen


def attend(carried, query_groups, query_req, query_tok, keys, values, key_req, key_tok):
    length = keys.shape[0]
    chosen = block_rows_for(length)
    blocks = length // chosen
    heads_here = query_groups.shape[1]
    score_scale = 1.0 / math.sqrt(HD)
    key_blocks = keys.reshape(blocks, chosen, heads_here, HD)
    value_blocks = values.reshape(blocks, chosen, heads_here, HD)
    req_blocks = key_req.reshape(blocks, chosen)
    tok_blocks = key_tok.reshape(blocks, chosen)

    def one_block(inner, items):
        running_max, running_sum, numerator = inner
        key_part, value_part, req_part, tok_part = items
        visible = (req_part[None, :] == query_req[:, None]) & (
            tok_part[None, :] <= query_tok[:, None]
        )
        scores = (
            jnp.einsum("tkgd,nkd->kgtn", query_groups, key_part, preferred_element_type=jnp.float32)
            * score_scale
        )
        scores = jnp.where(visible, scores, masked_score)
        new_max = jnp.maximum(running_max, jnp.max(scores, axis=-1))
        rescale = jnp.exp(running_max - new_max)
        weights = jnp.where(visible, jnp.exp(scores - new_max[..., None]), 0.0)
        running_sum = running_sum * rescale + jnp.sum(weights, axis=-1)
        numerator = numerator * rescale[..., None] + jnp.einsum(
            "kgtn,nkd->kgtd",
            weights.astype(jnp.bfloat16),
            value_part,
            preferred_element_type=jnp.float32,
        )
        return ((new_max, running_sum, numerator), None)

    result, ignored = lax.scan(
        one_block, carried, (key_blocks, value_blocks, req_blocks, tok_blocks)
    )
    return result


def maybe_attend(
    carried, query_groups, query_req, query_tok, summary, keys, values, key_req, key_tok
):
    query_has, query_last = summary
    request_ids = jnp.arange(query_has.shape[0], dtype=jnp.int32)
    matches = key_req[:, None] == request_ids[None, :]
    wanted = jnp.any(matches & query_has[None, :], axis=1)
    latest = jnp.max(jnp.where(matches, query_last[None, :], -2), axis=1)
    touched = jnp.any(wanted & (key_tok <= latest))
    return lax.cond(
        touched,
        lambda inner: attend(
            inner, query_groups, query_req, query_tok, keys, values, key_req, key_tok
        ),
        lambda inner: inner,
        carried,
    )


def any_cycle(
    queries,
    new_keys,
    new_values,
    prefix_keys,
    prefix_values,
    span_lens,
    prefix_lens,
    placement,
    decode_dest,
):
    cycle_size = lax.axis_size("blk")
    my_index = lax.axis_index("blk")
    rows_here = queries.shape[0]
    kv_cols = new_keys.shape[1]
    heads_here = kv_cols // HD
    groups = H // KVH
    query_groups = queries.reshape(rows_here, heads_here, groups, HD)
    query_tok = lax.dynamic_slice_in_dim(placement, my_index * rows_here, rows_here)
    query_req = request_of(query_tok, span_lens)
    token_req = request_of(placement, span_lens)
    prefix_total = prefix_keys.shape[0] * cycle_size
    prefix_req = request_of(jnp.arange(prefix_total, dtype=jnp.int32), prefix_lens)
    request_ids = jnp.arange(span_lens.shape[0], dtype=jnp.int32)
    member = query_req[:, None] == request_ids[None, :]
    summary = (jnp.any(member, axis=0), jnp.max(jnp.where(member, query_tok[:, None], -1), axis=0))
    initial = (
        jnp.full((heads_here, groups, rows_here), masked_score, jnp.float32),
        jnp.zeros((heads_here, groups, rows_here), jnp.float32),
        jnp.zeros((heads_here, groups, rows_here, HD), jnp.float32),
    )
    piece_keys = lax.all_gather(prefix_keys, "blk", axis=0, tiled=True)
    piece_values = lax.all_gather(prefix_values, "blk", axis=0, tiled=True)
    length = piece_keys.shape[0]
    key_req = prefix_req
    key_tok = jnp.full((length,), -1, jnp.int32)
    carried = maybe_attend(
        initial,
        query_groups,
        query_req,
        query_tok,
        summary,
        piece_keys,
        piece_values,
        key_req,
        key_tok,
    )
    destination = decode_dest[:, 0]
    capacity = 2 * rows_here // cycle_size
    piece_keys = lax.all_gather(new_keys, "blk", axis=0, tiled=True)
    piece_values = lax.all_gather(new_values, "blk", axis=0, tiled=True)
    key_req = token_req
    key_tok = placement
    carried = maybe_attend(
        carried,
        query_groups,
        query_req,
        query_tok,
        summary,
        piece_keys,
        piece_values,
        key_req,
        key_tok,
    )
    local_dest = lax.dynamic_slice_in_dim(destination, my_index * rows_here, rows_here)
    one_hot = (local_dest[:, None] == jnp.arange(cycle_size, dtype=jnp.int32)[None, :]).astype(
        jnp.int32
    )
    slot_rank = jnp.sum(jnp.cumsum(one_hot, axis=0) * one_hot, axis=1) - 1
    target = local_dest * capacity + slot_rank
    selector = (
        jnp.arange(cycle_size * capacity, dtype=jnp.int32)[:, None] == target[None, :]
    ).astype(jnp.bfloat16)
    stacked = jnp.concatenate([new_keys, new_values], axis=1)
    outgoing = jnp.dot(selector, stacked, preferred_element_type=jnp.float32).astype(jnp.bfloat16)
    moved = lax.all_to_all(outgoing, "blk", split_axis=0, concat_axis=0, tiled=True)
    running_max, running_sum, numerator = carried
    attended = (
        (numerator / running_sum[..., None])
        .transpose(2, 0, 1, 3)
        .reshape(rows_here, heads_here * groups * HD)
        .astype(jnp.bfloat16)
    )
    return (attended, moved[:, :kv_cols], moved[:, kv_cols:])


def solution(mesh):
    rows = P(("groups", "blk"), "tensor")
    return jax.shard_map(
        cycle_of_eight if mesh.shape["blk"] == 8 else any_cycle,
        mesh=mesh,
        in_specs=(rows,) * 5 + (P("groups"),) * 3 + (P("groups", None),),
        out_specs=(rows,) * 3,
        check_vma=False,
    )
```

```python
import functools
import math

import jax
import jax.numpy as jnp
from jax import lax
from jax.experimental import pallas as pl
from jax.experimental.pallas import tpu as pltpu
from jax.sharding import PartitionSpec as P

H = 64
KVH = 8
HD = 128
PIECE = 64
LARGE_NEGATIVE = -1e30

VMEM = pltpu.VMEM
SMEM = pltpu.SMEM
HBM = pltpu.HBM


def dot_nt(a, b):
    return lax.dot_general(a, b, (((1,), (1,)), ((), ())), preferred_element_type=jnp.float32)


def dot_nn(a, b):
    return lax.dot_general(a, b, (((1,), (0,)), ((), ())), preferred_element_type=jnp.float32)


def part_of(block, which, rows, start, size):
    if len(block) == 1:
        return block[0][which * rows:(which + 1) * rows, start:start + size]
    half, inner = divmod(which, 2)
    return block[half][inner * rows:(inner + 1) * rows, start:start + size]


def add_blocks(blocks, biases, query_ref, before, after, heads, groups, store):
    rows = query_ref.shape[0]
    factor = math.log2(math.e) / math.sqrt(HD)
    step = 2
    for k in range(heads):
        keys, values = [], []
        for block in blocks:
            keys.append(
                jnp.concatenate(
                    [part_of(block, j, rows, k * HD, HD) for j in (0, 2)], axis=0
                )
            )
            value = jnp.concatenate(
                [part_of(block, j, rows, k * HD, HD) for j in (1, 3)], axis=0
            )
            values.append(jnp.concatenate([value, jnp.ones_like(value)], axis=1))
        for g in range(0, groups, step):
            query = jnp.concatenate(
                [
                    query_ref[:, (k * groups + g + j) * HD:(k * groups + g + j + 1) * HD]
                    for j in range(step)
                ],
                axis=0,
            )
            at = slice(g * rows, (g + step) * rows)
            scores = []
            for key, bias in zip(keys, biases):
                score = (dot_nt(query, key) * factor).reshape(step, rows, 2 * rows) + bias[...][None]
                scores.append(score.reshape(step * rows, 2 * rows))
            largest = functools.reduce(jnp.maximum, scores)
            new_max = jnp.broadcast_to(
                jnp.max(largest, axis=1, keepdims=True), (step * rows, HD)
            )
            if before is not None:
                old_max = before[0][k, at, :]
                new_max = jnp.maximum(old_max, new_max)
            both_max = jnp.concatenate([new_max, new_max], axis=1)
            added = None
            for score, value in zip(scores, values):
                weights = jnp.exp2(score - both_max).astype(jnp.bfloat16)
                term = dot_nn(weights, value)
                added = term if added is None else added + term
            if before is not None:
                rescale = jnp.exp2(old_max - new_max)
                rescale = jnp.concatenate([rescale, rescale], axis=1)
                added = before[1][k, at, :] * rescale + added
            if after is not None:
                after[0][k, at, :] = new_max
                after[1][k, at, :] = added
            else:
                for j in range(step):
                    both = added[j * rows:(j + 1) * rows]
                    store(k, g + j, both[:, :HD] / both[:, HD:])
        if after is None:
            store(k, None, None)


def pick_rows(offsets, blocks, choose_refs, out_refs, picked_ref, sems):
    me = lax.axis_index("blk")
    copies = []
    for n, (offset, block, choose_ref) in enumerate(zip(offsets, blocks, choose_refs)):
        capacity, rows = choose_ref.shape
        index = me ^ offset
        for which, out_ref in enumerate(out_refs):
            new = part_of(block, 2 + which, rows, 0, out_ref.shape[1])
            picked_ref[n, which] = dot_nn(choose_ref[...], new).astype(jnp.bfloat16)
            copy = pltpu.make_async_copy(
                picked_ref.at[n, which],
                out_ref.at[pl.ds(pl.multiple_of(index * capacity, capacity), capacity)],
                sems.at[n, which],
            )
            copy.start()
            copies.append(copy)
    return copies


def first_kernel(
    offsets, rows, heads, groups, requests, capacity,
    place_in, span_in, plen_in, dest_in, query_in, own_ref,
    max_ref, acc_ref, dkey_ref, dval_ref, query_ref, bias_ref, choose_ref,
    place_ref, span_ref, plen_ref, dest_ref, picked_ref, sems, small_sems,
):
    small = [
        pltpu.make_async_copy(source, target, small_sems.at[j])
        for j, (source, target) in enumerate(
            (
                (place_in, place_ref),
                (span_in, span_ref),
                (plen_in, plen_ref),
                (dest_in, dest_ref),
                (query_in, query_ref),
            )
        )
    ]
    for copy in small:
        copy.start()
    for copy in small:
        copy.wait()
    me = lax.axis_index("blk")
    pieces = rows // PIECE

    def bounds(token):
        low = jnp.zeros_like(token)
        pre_low = jnp.zeros_like(token)
        pre_high = jnp.zeros_like(token) + plen_ref[0]
        end = jnp.int32(0)
        for r in range(requests - 1):
            end = end + span_ref[r]
            past = token >= end
            low = low + jnp.where(past, span_ref[r], 0)
            pre_low = pre_low + jnp.where(past, plen_ref[r], 0)
            pre_high = pre_high + jnp.where(past, plen_ref[r + 1], 0)
        return low, pre_low, pre_high

    def tokens_of(index, shape, axis):
        place = lax.broadcasted_iota(jnp.int32, shape, axis)
        token = place
        for piece in range(pieces):
            start = place_ref[index * rows + piece * PIECE] - piece * PIECE
            token = jnp.where(place >= piece * PIECE, place + start, token)
        return token

    token = tokens_of(me, (rows, rows), 0)
    low, pre_low, pre_high = bounds(token)
    column = lax.broadcasted_iota(jnp.int32, (rows, rows), 1)
    earlier = jnp.where(lax.broadcasted_iota(jnp.int32, (rows, rows), 0) < column, 1.0, 0.0)
    earlier = earlier.astype(jnp.bfloat16)
    slot = lax.broadcasted_iota(jnp.int32, (capacity, rows), 0).astype(jnp.float32)
    for n, offset in enumerate(offsets):
        index = me ^ offset
        position = column + index * rows
        pre_seen = (position >= pre_low) & (position < pre_high)
        key_token = tokens_of(index, (rows, rows), 1)
        new_seen = (key_token >= low) & (key_token <= token)
        bias_ref[n, :, :rows] = jnp.where(pre_seen, 0.0, LARGE_NEGATIVE).astype(jnp.float32)
        bias_ref[n, :, rows:] = jnp.where(new_seen, 0.0, LARGE_NEGATIVE).astype(jnp.float32)
        mine = jnp.where(dest_ref[pl.ds(index, 1), :] == me, 1.0, 0.0)
        mine = jnp.broadcast_to(mine, (capacity, rows))
        rank = dot_nn(mine.astype(jnp.bfloat16), earlier)
        choose_ref[n] = jnp.where((rank == slot) & (mine > 0.5), 1.0, 0.0).astype(jnp.bfloat16)
    copies = pick_rows(
        (0,), [[own_ref]], [choose_ref.at[0]], (dkey_ref, dval_ref), picked_ref, sems
    )
    add_blocks(
        [[own_ref]], [bias_ref.at[0]], query_ref, None, (max_ref, acc_ref), heads, groups, None
    )
    for copy in copies:
        copy.wait()


def stage_kernel(order, offsets, parts, last, heads, groups, *refs):
    refs = list(refs)
    query_ref, bias_ref, choose_ref = refs[:3]
    refs = refs[3:]
    blocks = []
    for count in parts:
        blocks.append(refs[:count])
        refs = refs[count:]
    before = refs[:2]
    refs = refs[4:]
    if last:
        att_ref, dkey_ref, dval_ref, picked_ref, sems, att_vmem, att_sems = refs
        after = None
    else:
        max_ref, acc_ref, dkey_ref, dval_ref, picked_ref, sems = refs
        after = (max_ref, acc_ref)
    copies = pick_rows(
        offsets, blocks, [choose_ref.at[n] for n in order], (dkey_ref, dval_ref), picked_ref, sems
    )

    def store(k, g, result):
        if g is not None:
            att_vmem[:, (k * groups + g) * HD:(k * groups + g + 1) * HD] = result.astype(jnp.bfloat16)
            return
        columns = slice(k * groups * HD, (k + 1) * groups * HD)
        copy = pltpu.make_async_copy(
            att_vmem.at[:, columns], att_ref.at[:, columns], att_sems.at[k]
        )
        copy.start()
        copies.append(copy)

    add_blocks(
        blocks, [bias_ref.at[n] for n in order], query_ref, before, after, heads, groups, store
    )
    for copy in copies:
        copy.wait()


def in_vmem(x):
    return pltpu.with_memory_space_constraint(x, VMEM)


def shapes_of(rows, columns, cycle):
    groups = H // KVH
    heads = columns // (groups * HD)
    state = (
        VMEM((heads, groups * rows, HD), jnp.float32),
        VMEM((heads, groups * rows, 2 * HD), jnp.float32),
    )
    decode = jax.ShapeDtypeStruct((2 * rows, heads * HD), jnp.bfloat16)
    return groups, heads, state, (decode, decode)


def params(keys, rows, columns):
    return dict(
        compiler_params=pltpu.CompilerParams(vmem_limit_bytes=20 * 1024 * 1024),
        cost_estimate=pl.CostEstimate(
            flops=4 * rows * columns * keys, bytes_accessed=4 * 1024 * 1024, transcendentals=0
        ),
    )


def run_first(small, query, own, offsets, capacity):
    rows, columns = query.shape
    cycle = len(offsets)
    groups, heads, state, decode = shapes_of(rows, columns, cycle)
    hbm, vmem = pl.BlockSpec(memory_space=HBM), pl.BlockSpec(memory_space=VMEM)
    small = tuple(pltpu.with_memory_space_constraint(x, HBM) for x in small)
    *state, dkey, dval, query, bias, choose = pl.pallas_call(
        functools.partial(
            first_kernel, offsets, rows, heads, groups, small[1].shape[0], capacity
        ),
        out_shape=(
            *state,
            *decode,
            VMEM((rows, columns), jnp.bfloat16),
            VMEM((cycle, rows, 2 * rows), jnp.float32),
            VMEM((cycle, capacity, rows), jnp.bfloat16),
        ),
        in_specs=[hbm] * 5 + [vmem],
        out_specs=(vmem, vmem, hbm, hbm, vmem, vmem, vmem),
        scratch_shapes=[
            *[SMEM(x.shape, jnp.int32) for x in small[:3]],
            VMEM(small[3].shape, jnp.int32),
            VMEM((1, 2, capacity, heads * HD), jnp.bfloat16),
            pltpu.SemaphoreType.DMA((1, 2)),
            pltpu.SemaphoreType.DMA((5,)),
        ],
        **params(2 * rows, rows, columns),
    )(*small, pltpu.with_memory_space_constraint(query, HBM), in_vmem(own))
    return [*state, dkey, dval], (query, bias, choose)


def run_stage(common, order, offsets, blocks, carry, last):
    rows, columns = common[0].shape
    cycle, capacity, unused = common[2].shape
    groups, heads, state, decode = shapes_of(rows, columns, cycle)
    parts = tuple(len(block) for block in blocks)
    flat = [in_vmem(ref) for block in blocks for ref in block]
    hbm, vmem = pl.BlockSpec(memory_space=HBM), pl.BlockSpec(memory_space=VMEM)
    operands = [*(in_vmem(x) for x in common), *flat]
    at = len(operands)
    operands += [in_vmem(carry[0]), in_vmem(carry[1]), *carry[2:]]
    scratch = [
        VMEM((len(blocks), 2, capacity, heads * HD), jnp.bfloat16),
        pltpu.SemaphoreType.DMA((len(blocks), 2)),
    ]
    if last:
        out_shape = (jax.ShapeDtypeStruct((rows, columns), jnp.bfloat16), *decode)
        out_specs = (hbm, hbm, hbm)
        alias = {at + 2: 1, at + 3: 2}
        scratch += [VMEM((rows, columns), jnp.bfloat16), pltpu.SemaphoreType.DMA((heads,))]
    else:
        out_shape = (*state, *decode)
        out_specs = (vmem, vmem, hbm, hbm)
        alias = {at + j: j for j in range(4)}
    return pl.pallas_call(
        functools.partial(stage_kernel, order, offsets, parts, last, heads, groups),
        out_shape=out_shape,
        in_specs=[vmem] * (at + 2) + [hbm] * 2,
        out_specs=out_specs,
        input_output_aliases=alias,
        scratch_shapes=scratch,
        **params(2 * rows * len(blocks), rows, columns),
    )(*operands)


def pack_kernel(*refs):
    *inputs, out_ref, sems = refs
    rows = inputs[0].shape[0]
    copies = [
        pltpu.make_async_copy(ref, out_ref.at[j * rows:(j + 1) * rows], sems.at[j])
        for j, ref in enumerate(inputs)
    ]
    for copy in copies:
        copy.start()
    for copy in copies:
        copy.wait()


def pack(*arrays):
    rows, columns = arrays[0].shape
    return pl.pallas_call(
        pack_kernel,
        out_shape=VMEM((rows * len(arrays), columns), jnp.bfloat16),
        in_specs=[pl.BlockSpec(memory_space=HBM)] * len(arrays),
        out_specs=pl.BlockSpec(memory_space=VMEM),
        scratch_shapes=[pltpu.SemaphoreType.DMA((len(arrays),))],
        compiler_params=pltpu.CompilerParams(vmem_limit_bytes=4 * 1024 * 1024),
    )(*(pltpu.with_memory_space_constraint(x, HBM) for x in arrays))


def choose_kernel(at_ends, between, *refs):
    out_ref = refs[-1]
    place = lax.axis_index("blk") // 2
    outer = (place == 0) | (place == 3)

    @pl.when(outer)
    def _():
        out_ref[...] = at_ends[...]

    @pl.when(jnp.logical_not(outer))
    def _():
        out_ref[...] = between[...]


def choose(at_ends, between, *after):
    vmem = pl.BlockSpec(memory_space=VMEM)
    return pl.pallas_call(
        choose_kernel,
        out_shape=VMEM(at_ends.shape, at_ends.dtype),
        in_specs=[vmem] * (2 + len(after)),
        out_specs=vmem,
        compiler_params=pltpu.CompilerParams(vmem_limit_bytes=8 * 1024 * 1024),
    )(in_vmem(at_ends), in_vmem(between), *(in_vmem(x) for x in after))


def half_kernel(which, in_ref, *refs):
    out_ref = refs[-1]
    rows = out_ref.shape[0]
    out_ref[...] = in_ref[which * rows:(which + 1) * rows]


def half_of(x, which, *after):
    vmem = pl.BlockSpec(memory_space=VMEM)
    return pl.pallas_call(
        functools.partial(half_kernel, which),
        out_shape=VMEM((x.shape[0] // 2, x.shape[1]), x.dtype),
        in_specs=[vmem] * (1 + len(after)),
        out_specs=vmem,
        compiler_params=pltpu.CompilerParams(vmem_limit_bytes=8 * 1024 * 1024),
    )(in_vmem(x), *(in_vmem(y) for y in after))


def together(values, *after):
    return lax.optimization_barrier(tuple(values) + after)[: len(values)]


def cycle_of_eight(
    queries, new_keys, new_values, prefix_keys, prefix_values, span_lens, prefix_lens, placement, decode_dest
):
    cycle = lax.axis_size("blk")
    rows = queries.shape[0]
    capacity = 2 * rows // cycle

    def moves(table):
        return [(2 * a + y, 2 * b + y) for a, b in table.items() for y in range(2)]

    swap = [(i, i ^ 1) for i in range(cycle)]
    near = moves({0: 1, 1: 0, 2: 3, 3: 2})
    middle = moves({1: 2, 2: 1})
    ends = moves({0: 3, 3: 0})
    skip = moves({0: 2, 3: 1, 2: 3, 1: 0})
    send = lambda x, table: lax.ppermute(x, "blk", table)

    small = (placement, span_lens, prefix_lens, decode_dest.reshape(cycle, rows))
    own = pack(prefix_keys, prefix_values, new_keys, new_values)
    half = own.shape[0] // 2

    offsets = (0, 2, 1, 6, 3, 4, 7, 5)

    a = send(own, near)
    y_own = send(own, swap)
    b_inner = send(own, middle)
    carry, common = run_first(small, queries, own, offsets, capacity)

    own_2, *carry = together((choose(own, own, a), *carry))
    b_outer = send(own_2, ends)
    a_2, *carry = together((choose(a, a, y_own, own_2), *carry))
    y_a = send(a_2, swap)
    carry = run_stage(common, (1, 2), offsets[1:3], [[a], [y_own]], carry, False)

    skip_from, *carry = together((choose(own, b_inner, b_outer), *carry))
    c = send(skip_from, skip)
    b_outer, *carry = together((b_outer, *carry), skip_from)
    b = choose(b_outer, b_inner, y_a)
    y_b = send(b, swap)
    carry = run_stage(common, (3, 4), offsets[3:5], [[b], [y_a]], carry, False)

    c_low = half_of(c, 0, carry[0])
    y_c_low = send(c_low, swap)
    y_b_high, *carry = together((half_of(y_b, 1, c_low), *carry))
    y_c_high = send(y_b_high, near)
    carry = run_stage(common, (5, 6), offsets[5:7], [[c], [y_b]], carry, False)
    return tuple(run_stage(common, (7,), offsets[7:], [[choose(y_c_low, y_c_low), y_c_high]], carry, True))


masked_score = -1e30


def request_of(index, lens):
    ends = jnp.cumsum(lens)
    return jnp.sum((index[:, None] >= ends[None, :]).astype(jnp.int32), axis=1)


def block_rows_for(length):
    chosen = 512
    while length % chosen:
        chosen = chosen // 2
    return chosen


def attend(carried, query_groups, query_req, query_tok, keys, values, key_req, key_tok):
    length = keys.shape[0]
    chosen = block_rows_for(length)
    blocks = length // chosen
    heads_here = query_groups.shape[1]
    score_scale = 1.0 / math.sqrt(HD)
    key_blocks = keys.reshape(blocks, chosen, heads_here, HD)
    value_blocks = values.reshape(blocks, chosen, heads_here, HD)
    req_blocks = key_req.reshape(blocks, chosen)
    tok_blocks = key_tok.reshape(blocks, chosen)

    def one_block(inner, items):
        running_max, running_sum, numerator = inner
        key_part, value_part, req_part, tok_part = items
        visible = (req_part[None, :] == query_req[:, None]) & (
            tok_part[None, :] <= query_tok[:, None]
        )
        scores = (
            jnp.einsum("tkgd,nkd->kgtn", query_groups, key_part, preferred_element_type=jnp.float32)
            * score_scale
        )
        scores = jnp.where(visible, scores, masked_score)
        new_max = jnp.maximum(running_max, jnp.max(scores, axis=-1))
        rescale = jnp.exp(running_max - new_max)
        weights = jnp.where(visible, jnp.exp(scores - new_max[..., None]), 0.0)
        running_sum = running_sum * rescale + jnp.sum(weights, axis=-1)
        numerator = numerator * rescale[..., None] + jnp.einsum(
            "kgtn,nkd->kgtd",
            weights.astype(jnp.bfloat16),
            value_part,
            preferred_element_type=jnp.float32,
        )
        return ((new_max, running_sum, numerator), None)

    result, ignored = lax.scan(
        one_block, carried, (key_blocks, value_blocks, req_blocks, tok_blocks)
    )
    return result


def maybe_attend(
    carried, query_groups, query_req, query_tok, summary, keys, values, key_req, key_tok
):
    query_has, query_last = summary
    request_ids = jnp.arange(query_has.shape[0], dtype=jnp.int32)
    matches = key_req[:, None] == request_ids[None, :]
    wanted = jnp.any(matches & query_has[None, :], axis=1)
    latest = jnp.max(jnp.where(matches, query_last[None, :], -2), axis=1)
    touched = jnp.any(wanted & (key_tok <= latest))
    return lax.cond(
        touched,
        lambda inner: attend(
            inner, query_groups, query_req, query_tok, keys, values, key_req, key_tok
        ),
        lambda inner: inner,
        carried,
    )


def any_cycle(
    queries,
    new_keys,
    new_values,
    prefix_keys,
    prefix_values,
    span_lens,
    prefix_lens,
    placement,
    decode_dest,
):
    cycle_size = lax.axis_size("blk")
    my_index = lax.axis_index("blk")
    rows_here = queries.shape[0]
    kv_cols = new_keys.shape[1]
    heads_here = kv_cols // HD
    groups = H // KVH
    query_groups = queries.reshape(rows_here, heads_here, groups, HD)
    query_tok = lax.dynamic_slice_in_dim(placement, my_index * rows_here, rows_here)
    query_req = request_of(query_tok, span_lens)
    token_req = request_of(placement, span_lens)
    prefix_total = prefix_keys.shape[0] * cycle_size
    prefix_req = request_of(jnp.arange(prefix_total, dtype=jnp.int32), prefix_lens)
    request_ids = jnp.arange(span_lens.shape[0], dtype=jnp.int32)
    member = query_req[:, None] == request_ids[None, :]
    summary = (jnp.any(member, axis=0), jnp.max(jnp.where(member, query_tok[:, None], -1), axis=0))
    initial = (
        jnp.full((heads_here, groups, rows_here), masked_score, jnp.float32),
        jnp.zeros((heads_here, groups, rows_here), jnp.float32),
        jnp.zeros((heads_here, groups, rows_here, HD), jnp.float32),
    )
    piece_keys = lax.all_gather(prefix_keys, "blk", axis=0, tiled=True)
    piece_values = lax.all_gather(prefix_values, "blk", axis=0, tiled=True)
    length = piece_keys.shape[0]
    key_req = prefix_req
    key_tok = jnp.full((length,), -1, jnp.int32)
    carried = maybe_attend(
        initial,
        query_groups,
        query_req,
        query_tok,
        summary,
        piece_keys,
        piece_values,
        key_req,
        key_tok,
    )
    destination = decode_dest[:, 0]
    capacity = 2 * rows_here // cycle_size
    piece_keys = lax.all_gather(new_keys, "blk", axis=0, tiled=True)
    piece_values = lax.all_gather(new_values, "blk", axis=0, tiled=True)
    key_req = token_req
    key_tok = placement
    carried = maybe_attend(
        carried,
        query_groups,
        query_req,
        query_tok,
        summary,
        piece_keys,
        piece_values,
        key_req,
        key_tok,
    )
    local_dest = lax.dynamic_slice_in_dim(destination, my_index * rows_here, rows_here)
    one_hot = (local_dest[:, None] == jnp.arange(cycle_size, dtype=jnp.int32)[None, :]).astype(
        jnp.int32
    )
    slot_rank = jnp.sum(jnp.cumsum(one_hot, axis=0) * one_hot, axis=1) - 1
    target = local_dest * capacity + slot_rank
    selector = (
        jnp.arange(cycle_size * capacity, dtype=jnp.int32)[:, None] == target[None, :]
    ).astype(jnp.bfloat16)
    stacked = jnp.concatenate([new_keys, new_values], axis=1)
    outgoing = jnp.dot(selector, stacked, preferred_element_type=jnp.float32).astype(jnp.bfloat16)
    moved = lax.all_to_all(outgoing, "blk", split_axis=0, concat_axis=0, tiled=True)
    running_max, running_sum, numerator = carried
    attended = (
        (numerator / running_sum[..., None])
        .transpose(2, 0, 1, 3)
        .reshape(rows_here, heads_here * groups * HD)
        .astype(jnp.bfloat16)
    )
    return (attended, moved[:, :kv_cols], moved[:, kv_cols:])


def solution(mesh):
    rows = P(("groups", "blk"), "tensor")
    return jax.shard_map(
        cycle_of_eight if mesh.shape["blk"] == 8 else any_cycle,
        mesh=mesh,
        in_specs=(rows,) * 5 + (P("groups"),) * 3 + (P("groups", None),),
        out_specs=(rows,) * 3,
        check_vma=False,
    )
```

```python
import functools
import math

import jax
import jax.numpy as jnp
from jax import lax
from jax.experimental import pallas as pl
from jax.experimental.pallas import tpu as pltpu
from jax.sharding import PartitionSpec as P

H = 64
KVH = 8
HD = 128
PIECE = 64
LARGE_NEGATIVE = -1e30

VMEM = pltpu.VMEM
SMEM = pltpu.SMEM
HBM = pltpu.HBM


def dot_nt(a, b):
    return lax.dot_general(a, b, (((1,), (1,)), ((), ())), preferred_element_type=jnp.float32)


def dot_nn(a, b):
    return lax.dot_general(a, b, (((1,), (0,)), ((), ())), preferred_element_type=jnp.float32)


def part_of(block, which, rows, start, size):
    first, stop, found = which * rows, (which + 1) * rows, []
    for part in block:
        length = part.shape[0]
        if first < min(stop, length):
            found.append(part[first:min(stop, length), start:start + size])
        first, stop = max(first - length, 0), stop - length
    return found[0] if len(found) == 1 else jnp.concatenate(found, axis=0)


def add_blocks(blocks, biases, query_ref, before, after, heads, groups, store):
    rows = query_ref.shape[0]
    factor = math.log2(math.e) / math.sqrt(HD)
    step = 2
    for k in range(heads):
        keys, values = [], []
        for block in blocks:
            keys.append(
                jnp.concatenate(
                    [part_of(block, j, rows, k * HD, HD) for j in (0, 2)], axis=0
                )
            )
            value = jnp.concatenate(
                [part_of(block, j, rows, k * HD, HD) for j in (1, 3)], axis=0
            )
            values.append(jnp.concatenate([value, jnp.ones_like(value)], axis=1))
        for g in range(0, groups, step):
            query = jnp.concatenate(
                [
                    query_ref[:, (k * groups + g + j) * HD:(k * groups + g + j + 1) * HD]
                    for j in range(step)
                ],
                axis=0,
            )
            at = slice(g * rows, (g + step) * rows)
            scores = []
            for key, bias in zip(keys, biases):
                score = (dot_nt(query, key) * factor).reshape(step, rows, 2 * rows) + bias[...][None]
                scores.append(score.reshape(step * rows, 2 * rows))
            largest = functools.reduce(jnp.maximum, scores)
            new_max = jnp.broadcast_to(
                jnp.max(largest, axis=1, keepdims=True), (step * rows, HD)
            )
            if before is not None:
                old_max = before[0][k, at, :]
                new_max = jnp.maximum(old_max, new_max)
            both_max = jnp.concatenate([new_max, new_max], axis=1)
            added = None
            for score, value in zip(scores, values):
                weights = jnp.exp2(score - both_max).astype(jnp.bfloat16)
                term = dot_nn(weights, value)
                added = term if added is None else added + term
            if before is not None:
                rescale = jnp.exp2(old_max - new_max)
                rescale = jnp.concatenate([rescale, rescale], axis=1)
                added = before[1][k, at, :] * rescale + added
            if after is not None:
                after[0][k, at, :] = new_max
                after[1][k, at, :] = added
            else:
                for j in range(step):
                    both = added[j * rows:(j + 1) * rows]
                    store(k, g + j, both[:, :HD] / both[:, HD:])
        if after is None:
            store(k, None, None)


def pick_rows(offsets, blocks, choose_refs, out_refs, picked_ref, sems):
    me = lax.axis_index("blk")
    copies = []
    for n, (offset, block, choose_ref) in enumerate(zip(offsets, blocks, choose_refs)):
        capacity, rows = choose_ref.shape
        index = me ^ offset
        for which, out_ref in enumerate(out_refs):
            new = part_of(block, 2 + which, rows, 0, out_ref.shape[1])
            picked_ref[n, which] = dot_nn(choose_ref[...], new).astype(jnp.bfloat16)
            copy = pltpu.make_async_copy(
                picked_ref.at[n, which],
                out_ref.at[pl.ds(pl.multiple_of(index * capacity, capacity), capacity)],
                sems.at[n, which],
            )
            copy.start()
            copies.append(copy)
    return copies


def first_kernel(
    offsets, rows, heads, groups, requests, capacity,
    place_in, span_in, plen_in, dest_in, query_in, own_ref,
    max_ref, acc_ref, dkey_ref, dval_ref, query_ref, bias_ref, choose_ref,
    place_ref, span_ref, plen_ref, dest_ref, picked_ref, sems, small_sems,
):
    small = [
        pltpu.make_async_copy(source, target, small_sems.at[j])
        for j, (source, target) in enumerate(
            (
                (place_in, place_ref),
                (span_in, span_ref),
                (plen_in, plen_ref),
                (dest_in, dest_ref),
                (query_in, query_ref),
            )
        )
    ]
    for copy in small:
        copy.start()
    for copy in small:
        copy.wait()
    me = lax.axis_index("blk")
    pieces = rows // PIECE

    def bounds(token):
        low = jnp.zeros_like(token)
        pre_low = jnp.zeros_like(token)
        pre_high = jnp.zeros_like(token) + plen_ref[0]
        end = jnp.int32(0)
        for r in range(requests - 1):
            end = end + span_ref[r]
            past = token >= end
            low = low + jnp.where(past, span_ref[r], 0)
            pre_low = pre_low + jnp.where(past, plen_ref[r], 0)
            pre_high = pre_high + jnp.where(past, plen_ref[r + 1], 0)
        return low, pre_low, pre_high

    def tokens_of(index, shape, axis):
        place = lax.broadcasted_iota(jnp.int32, shape, axis)
        token = place
        for piece in range(pieces):
            start = place_ref[index * rows + piece * PIECE] - piece * PIECE
            token = jnp.where(place >= piece * PIECE, place + start, token)
        return token

    token = tokens_of(me, (rows, rows), 0)
    low, pre_low, pre_high = bounds(token)
    column = lax.broadcasted_iota(jnp.int32, (rows, rows), 1)
    earlier = jnp.where(lax.broadcasted_iota(jnp.int32, (rows, rows), 0) < column, 1.0, 0.0)
    earlier = earlier.astype(jnp.bfloat16)
    slot = lax.broadcasted_iota(jnp.int32, (capacity, rows), 0).astype(jnp.float32)
    for n, offset in enumerate(offsets):
        index = me ^ offset
        position = column + index * rows
        pre_seen = (position >= pre_low) & (position < pre_high)
        key_token = tokens_of(index, (rows, rows), 1)
        new_seen = (key_token >= low) & (key_token <= token)
        bias_ref[n, :, :rows] = jnp.where(pre_seen, 0.0, LARGE_NEGATIVE).astype(jnp.float32)
        bias_ref[n, :, rows:] = jnp.where(new_seen, 0.0, LARGE_NEGATIVE).astype(jnp.float32)
        mine = jnp.where(dest_ref[pl.ds(index, 1), :] == me, 1.0, 0.0)
        mine = jnp.broadcast_to(mine, (capacity, rows))
        rank = dot_nn(mine.astype(jnp.bfloat16), earlier)
        choose_ref[n] = jnp.where((rank == slot) & (mine > 0.5), 1.0, 0.0).astype(jnp.bfloat16)
    copies = pick_rows(
        (0,), [[own_ref]], [choose_ref.at[0]], (dkey_ref, dval_ref), picked_ref, sems
    )
    add_blocks(
        [[own_ref]], [bias_ref.at[0]], query_ref, None, (max_ref, acc_ref), heads, groups, None
    )
    for copy in copies:
        copy.wait()


def stage_kernel(order, offsets, parts, last, heads, groups, *refs):
    refs = list(refs)
    query_ref, bias_ref, choose_ref = refs[:3]
    refs = refs[3:]
    blocks = []
    for count in parts:
        blocks.append(refs[:count])
        refs = refs[count:]
    before = refs[:2]
    refs = refs[4:]
    if last:
        att_ref, dkey_ref, dval_ref, picked_ref, sems, att_vmem, att_sems = refs
        after = None
    else:
        max_ref, acc_ref, dkey_ref, dval_ref, picked_ref, sems = refs
        after = (max_ref, acc_ref)
    copies = pick_rows(
        offsets, blocks, [choose_ref.at[n] for n in order], (dkey_ref, dval_ref), picked_ref, sems
    )

    def store(k, g, result):
        if g is not None:
            att_vmem[:, (k * groups + g) * HD:(k * groups + g + 1) * HD] = result.astype(jnp.bfloat16)
            return
        columns = slice(k * groups * HD, (k + 1) * groups * HD)
        copy = pltpu.make_async_copy(
            att_vmem.at[:, columns], att_ref.at[:, columns], att_sems.at[k]
        )
        copy.start()
        copies.append(copy)

    add_blocks(
        blocks, [bias_ref.at[n] for n in order], query_ref, before, after, heads, groups, store
    )
    for copy in copies:
        copy.wait()


def in_vmem(x):
    return pltpu.with_memory_space_constraint(x, VMEM)


def shapes_of(rows, columns, cycle):
    groups = H // KVH
    heads = columns // (groups * HD)
    state = (
        VMEM((heads, groups * rows, HD), jnp.float32),
        VMEM((heads, groups * rows, 2 * HD), jnp.float32),
    )
    decode = jax.ShapeDtypeStruct((2 * rows, heads * HD), jnp.bfloat16)
    return groups, heads, state, (decode, decode)


def params(keys, rows, columns):
    return dict(
        compiler_params=pltpu.CompilerParams(vmem_limit_bytes=20 * 1024 * 1024),
        cost_estimate=pl.CostEstimate(
            flops=4 * rows * columns * keys, bytes_accessed=4 * 1024 * 1024, transcendentals=0
        ),
    )


def run_first(small, query, own, offsets, capacity):
    rows, columns = query.shape
    cycle = len(offsets)
    groups, heads, state, decode = shapes_of(rows, columns, cycle)
    hbm, vmem = pl.BlockSpec(memory_space=HBM), pl.BlockSpec(memory_space=VMEM)
    small = tuple(pltpu.with_memory_space_constraint(x, HBM) for x in small)
    *state, dkey, dval, query, bias, choose = pl.pallas_call(
        functools.partial(
            first_kernel, offsets, rows, heads, groups, small[1].shape[0], capacity
        ),
        out_shape=(
            *state,
            *decode,
            VMEM((rows, columns), jnp.bfloat16),
            VMEM((cycle, rows, 2 * rows), jnp.float32),
            VMEM((cycle, capacity, rows), jnp.bfloat16),
        ),
        in_specs=[hbm] * 5 + [vmem],
        out_specs=(vmem, vmem, hbm, hbm, vmem, vmem, vmem),
        scratch_shapes=[
            *[SMEM(x.shape, jnp.int32) for x in small[:3]],
            VMEM(small[3].shape, jnp.int32),
            VMEM((1, 2, capacity, heads * HD), jnp.bfloat16),
            pltpu.SemaphoreType.DMA((1, 2)),
            pltpu.SemaphoreType.DMA((5,)),
        ],
        **params(2 * rows, rows, columns),
    )(*small, pltpu.with_memory_space_constraint(query, HBM), in_vmem(own))
    return [*state, dkey, dval], (query, bias, choose)


def run_stage(common, order, offsets, blocks, carry, last):
    rows, columns = common[0].shape
    cycle, capacity, unused = common[2].shape
    groups, heads, state, decode = shapes_of(rows, columns, cycle)
    parts = tuple(len(block) for block in blocks)
    flat = [in_vmem(ref) for block in blocks for ref in block]
    hbm, vmem = pl.BlockSpec(memory_space=HBM), pl.BlockSpec(memory_space=VMEM)
    operands = [*(in_vmem(x) for x in common), *flat]
    at = len(operands)
    operands += [in_vmem(carry[0]), in_vmem(carry[1]), *carry[2:]]
    scratch = [
        VMEM((len(blocks), 2, capacity, heads * HD), jnp.bfloat16),
        pltpu.SemaphoreType.DMA((len(blocks), 2)),
    ]
    if last:
        out_shape = (jax.ShapeDtypeStruct((rows, columns), jnp.bfloat16), *decode)
        out_specs = (hbm, hbm, hbm)
        alias = {at + 2: 1, at + 3: 2}
        scratch += [VMEM((rows, columns), jnp.bfloat16), pltpu.SemaphoreType.DMA((heads,))]
    else:
        out_shape = (*state, *decode)
        out_specs = (vmem, vmem, hbm, hbm)
        alias = {at + j: j for j in range(4)}
    return pl.pallas_call(
        functools.partial(stage_kernel, order, offsets, parts, last, heads, groups),
        out_shape=out_shape,
        in_specs=[vmem] * (at + 2) + [hbm] * 2,
        out_specs=out_specs,
        input_output_aliases=alias,
        scratch_shapes=scratch,
        **params(2 * rows * len(blocks), rows, columns),
    )(*operands)


def pack_kernel(*refs):
    *inputs, out_ref, sems = refs
    rows = inputs[0].shape[0]
    copies = [
        pltpu.make_async_copy(ref, out_ref.at[j * rows:(j + 1) * rows], sems.at[j])
        for j, ref in enumerate(inputs)
    ]
    for copy in copies:
        copy.start()
    for copy in copies:
        copy.wait()


def pack(*arrays):
    rows, columns = arrays[0].shape
    return pl.pallas_call(
        pack_kernel,
        out_shape=VMEM((rows * len(arrays), columns), jnp.bfloat16),
        in_specs=[pl.BlockSpec(memory_space=HBM)] * len(arrays),
        out_specs=pl.BlockSpec(memory_space=VMEM),
        scratch_shapes=[pltpu.SemaphoreType.DMA((len(arrays),))],
        compiler_params=pltpu.CompilerParams(vmem_limit_bytes=4 * 1024 * 1024),
    )(*(pltpu.with_memory_space_constraint(x, HBM) for x in arrays))


def choose_kernel(at_ends, between, *refs):
    out_ref = refs[-1]
    place = lax.axis_index("blk") // 2
    outer = (place == 0) | (place == 3)

    @pl.when(outer)
    def _():
        out_ref[...] = at_ends[...]

    @pl.when(jnp.logical_not(outer))
    def _():
        out_ref[...] = between[...]


def choose(at_ends, between, *after):
    vmem = pl.BlockSpec(memory_space=VMEM)
    return pl.pallas_call(
        choose_kernel,
        out_shape=VMEM(at_ends.shape, at_ends.dtype),
        in_specs=[vmem] * (2 + len(after)),
        out_specs=vmem,
        compiler_params=pltpu.CompilerParams(vmem_limit_bytes=8 * 1024 * 1024),
    )(in_vmem(at_ends), in_vmem(between), *(in_vmem(x) for x in after))


def rows_kernel(first, in_ref, *refs):
    out_ref = refs[-1]
    out_ref[...] = in_ref[first:first + out_ref.shape[0]]


def rows_of(x, first, stop, *after):
    vmem = pl.BlockSpec(memory_space=VMEM)
    return pl.pallas_call(
        functools.partial(rows_kernel, first),
        out_shape=VMEM((stop - first, x.shape[1]), x.dtype),
        in_specs=[vmem] * (1 + len(after)),
        out_specs=vmem,
        compiler_params=pltpu.CompilerParams(vmem_limit_bytes=8 * 1024 * 1024),
    )(in_vmem(x), *(in_vmem(y) for y in after))


def together(values, *after):
    return lax.optimization_barrier(tuple(values) + after)[: len(values)]


def cycle_of_eight(
    queries, new_keys, new_values, prefix_keys, prefix_values, span_lens, prefix_lens, placement, decode_dest
):
    cycle = lax.axis_size("blk")
    rows = queries.shape[0]
    capacity = 2 * rows // cycle

    def moves(table):
        return [(2 * a + y, 2 * b + y) for a, b in table.items() for y in range(2)]

    swap = [(i, i ^ 1) for i in range(cycle)]
    near = moves({0: 1, 1: 0, 2: 3, 3: 2})
    middle = moves({1: 2, 2: 1})
    ends = moves({0: 3, 3: 0})
    skip = moves({0: 2, 3: 1, 2: 3, 1: 0})
    send = lambda x, table: lax.ppermute(x, "blk", table)

    small = (placement, span_lens, prefix_lens, decode_dest.reshape(cycle, rows))
    own = pack(prefix_keys, prefix_values, new_keys, new_values)
    cut = own.shape[0] * 9 // 32 * 2

    offsets = (0, 2, 1, 6, 3, 4, 7, 5)

    a = send(own, near)
    y_own = send(own, swap)
    b_inner = send(own, middle)
    carry, common = run_first(small, queries, own, offsets, capacity)

    own_2, *carry = together((choose(own, own, a), *carry))
    b_outer = send(own_2, ends)
    a_2, *carry = together((choose(a, a, y_own, own_2), *carry))
    y_a = send(a_2, swap)
    carry = run_stage(common, (1, 2), offsets[1:3], [[a], [y_own]], carry, False)

    skip_from, *carry = together((choose(own, b_inner, b_outer), *carry))
    c = send(skip_from, skip)
    b_outer, *carry = together((b_outer, *carry), skip_from)
    b = choose(b_outer, b_inner, y_a)
    y_b = send(b, swap)
    carry = run_stage(common, (3, 4), offsets[3:5], [[b], [y_a]], carry, False)

    c_low = rows_of(c, 0, cut, carry[0])
    y_c_low = send(c_low, swap)
    y_b_high, *carry = together((rows_of(y_b, cut, y_b.shape[0], c_low), *carry))
    y_c_high = send(y_b_high, near)
    carry = run_stage(common, (5, 6), offsets[5:7], [[c], [y_b]], carry, False)
    return tuple(run_stage(common, (7,), offsets[7:], [[choose(y_c_low, y_c_low), y_c_high]], carry, True))


masked_score = -1e30


def request_of(index, lens):
    ends = jnp.cumsum(lens)
    return jnp.sum((index[:, None] >= ends[None, :]).astype(jnp.int32), axis=1)


def block_rows_for(length):
    chosen = 512
    while length % chosen:
        chosen = chosen // 2
    return chosen


def attend(carried, query_groups, query_req, query_tok, keys, values, key_req, key_tok):
    length = keys.shape[0]
    chosen = block_rows_for(length)
    blocks = length // chosen
    heads_here = query_groups.shape[1]
    score_scale = 1.0 / math.sqrt(HD)
    key_blocks = keys.reshape(blocks, chosen, heads_here, HD)
    value_blocks = values.reshape(blocks, chosen, heads_here, HD)
    req_blocks = key_req.reshape(blocks, chosen)
    tok_blocks = key_tok.reshape(blocks, chosen)

    def one_block(inner, items):
        running_max, running_sum, numerator = inner
        key_part, value_part, req_part, tok_part = items
        visible = (req_part[None, :] == query_req[:, None]) & (
            tok_part[None, :] <= query_tok[:, None]
        )
        scores = (
            jnp.einsum("tkgd,nkd->kgtn", query_groups, key_part, preferred_element_type=jnp.float32)
            * score_scale
        )
        scores = jnp.where(visible, scores, masked_score)
        new_max = jnp.maximum(running_max, jnp.max(scores, axis=-1))
        rescale = jnp.exp(running_max - new_max)
        weights = jnp.where(visible, jnp.exp(scores - new_max[..., None]), 0.0)
        running_sum = running_sum * rescale + jnp.sum(weights, axis=-1)
        numerator = numerator * rescale[..., None] + jnp.einsum(
            "kgtn,nkd->kgtd",
            weights.astype(jnp.bfloat16),
            value_part,
            preferred_element_type=jnp.float32,
        )
        return ((new_max, running_sum, numerator), None)

    result, ignored = lax.scan(
        one_block, carried, (key_blocks, value_blocks, req_blocks, tok_blocks)
    )
    return result


def maybe_attend(
    carried, query_groups, query_req, query_tok, summary, keys, values, key_req, key_tok
):
    query_has, query_last = summary
    request_ids = jnp.arange(query_has.shape[0], dtype=jnp.int32)
    matches = key_req[:, None] == request_ids[None, :]
    wanted = jnp.any(matches & query_has[None, :], axis=1)
    latest = jnp.max(jnp.where(matches, query_last[None, :], -2), axis=1)
    touched = jnp.any(wanted & (key_tok <= latest))
    return lax.cond(
        touched,
        lambda inner: attend(
            inner, query_groups, query_req, query_tok, keys, values, key_req, key_tok
        ),
        lambda inner: inner,
        carried,
    )


def any_cycle(
    queries,
    new_keys,
    new_values,
    prefix_keys,
    prefix_values,
    span_lens,
    prefix_lens,
    placement,
    decode_dest,
):
    cycle_size = lax.axis_size("blk")
    my_index = lax.axis_index("blk")
    rows_here = queries.shape[0]
    kv_cols = new_keys.shape[1]
    heads_here = kv_cols // HD
    groups = H // KVH
    query_groups = queries.reshape(rows_here, heads_here, groups, HD)
    query_tok = lax.dynamic_slice_in_dim(placement, my_index * rows_here, rows_here)
    query_req = request_of(query_tok, span_lens)
    token_req = request_of(placement, span_lens)
    prefix_total = prefix_keys.shape[0] * cycle_size
    prefix_req = request_of(jnp.arange(prefix_total, dtype=jnp.int32), prefix_lens)
    request_ids = jnp.arange(span_lens.shape[0], dtype=jnp.int32)
    member = query_req[:, None] == request_ids[None, :]
    summary = (jnp.any(member, axis=0), jnp.max(jnp.where(member, query_tok[:, None], -1), axis=0))
    initial = (
        jnp.full((heads_here, groups, rows_here), masked_score, jnp.float32),
        jnp.zeros((heads_here, groups, rows_here), jnp.float32),
        jnp.zeros((heads_here, groups, rows_here, HD), jnp.float32),
    )
    piece_keys = lax.all_gather(prefix_keys, "blk", axis=0, tiled=True)
    piece_values = lax.all_gather(prefix_values, "blk", axis=0, tiled=True)
    length = piece_keys.shape[0]
    key_req = prefix_req
    key_tok = jnp.full((length,), -1, jnp.int32)
    carried = maybe_attend(
        initial,
        query_groups,
        query_req,
        query_tok,
        summary,
        piece_keys,
        piece_values,
        key_req,
        key_tok,
    )
    destination = decode_dest[:, 0]
    capacity = 2 * rows_here // cycle_size
    piece_keys = lax.all_gather(new_keys, "blk", axis=0, tiled=True)
    piece_values = lax.all_gather(new_values, "blk", axis=0, tiled=True)
    key_req = token_req
    key_tok = placement
    carried = maybe_attend(
        carried,
        query_groups,
        query_req,
        query_tok,
        summary,
        piece_keys,
        piece_values,
        key_req,
        key_tok,
    )
    local_dest = lax.dynamic_slice_in_dim(destination, my_index * rows_here, rows_here)
    one_hot = (local_dest[:, None] == jnp.arange(cycle_size, dtype=jnp.int32)[None, :]).astype(
        jnp.int32
    )
    slot_rank = jnp.sum(jnp.cumsum(one_hot, axis=0) * one_hot, axis=1) - 1
    target = local_dest * capacity + slot_rank
    selector = (
        jnp.arange(cycle_size * capacity, dtype=jnp.int32)[:, None] == target[None, :]
    ).astype(jnp.bfloat16)
    stacked = jnp.concatenate([new_keys, new_values], axis=1)
    outgoing = jnp.dot(selector, stacked, preferred_element_type=jnp.float32).astype(jnp.bfloat16)
    moved = lax.all_to_all(outgoing, "blk", split_axis=0, concat_axis=0, tiled=True)
    running_max, running_sum, numerator = carried
    attended = (
        (numerator / running_sum[..., None])
        .transpose(2, 0, 1, 3)
        .reshape(rows_here, heads_here * groups * HD)
        .astype(jnp.bfloat16)
    )
    return (attended, moved[:, :kv_cols], moved[:, kv_cols:])


def solution(mesh):
    rows = P(("groups", "blk"), "tensor")
    return jax.shard_map(
        cycle_of_eight if mesh.shape["blk"] == 8 else any_cycle,
        mesh=mesh,
        in_specs=(rows,) * 5 + (P("groups"),) * 3 + (P("groups", None),),
        out_specs=(rows,) * 3,
        check_vma=False,
    )
```
